512 devices in a mesh: user: 16 (over y, core), dev: 32 (over z, x).
Axes of the slice: x: 4, y: 8, z: 8, core: 2. Of those that a mesh axis runs over, the one named last changes fastest.
Arguments:
- queries: bfloat16 [16384, 2048], P(('user', 'dev')), parts along dimension 0, may hold values from -9 to 9
- keys: bfloat16 [64, 256, 2048], P('user', 'dev'), parts along dimension 0, may hold values from -9 to 9
- values: bfloat16 [64, 256, 2048], P('user', 'dev'), parts along dimension 0, may hold values from -24 to 24
- kv_count: int32 [64, 32], P('user'), parts along dimension 0, may hold values from 1 to 8, 192 in all within a row
- beam_user: int32 [512], P('user'), parts along dimension 0, may hold values from 0 to 3, as said below
- routes: int32 [16384, 2], P(('user', 'dev')), parts along dimension 0, may hold values from 0 to 31, as said below
- route_gate: float32 [16384, 2], P(('user', 'dev')), parts along dimension 0, may hold values from 0.2 to 1
- norm_gain: float32 [2048], replicated, may hold values from 0.1 to 1.9
- w_up: bfloat16 [2048, 16384], P(None, 'dev'), may hold values from -0.125 to 0.125
- w_down: bfloat16 [16384, 2048], P('dev'), may hold values from -0.0625 to 0.0625
Outputs:
- context: bfloat16 [16384, 2048], P(('user', 'dev')), parts along dimension 0
- routed: bfloat16 [16384, 2048], P(('user', 'dev')), parts along dimension 0
The draws below stay inside these ranges and needn't reach their ends.
There are 16 independent parts, one for each index of `user`. The reference program is written for one: setup_inputs(seed, part) draws one part's arguments, and reference() takes and returns one part's arrays. A program takes and returns all parts, laid end to end along the dimension named above; an argument that names none is the same for every part. Nothing has to cross between parts.
Inputs may be any that keep to these rules, and one draw needn't show every extreme that they name: `beam_user`: each user owns the beams of exactly 8 devices. `routes`: each row names two different experts. On the rows of one device each expert 0 to 1 is named at most 16 times, and on every device one of them exactly 16 times.
All inputs are finite; a program needn't handle non-finite values.
Results may differ from the reference program's by a relative error of at most 0.012.
Values may be sent and summed in bfloat16 or wider, within the bound.
No kernel may reach another device: no remote copies, remote signals or barrier semaphores. Data moves between devices by JAX's collectives and lax.ppermute only.
A program may use at most 64 MiB of HBM per device.

```python
import math
import jax
import jax.numpy as jnp
import numpy as np
from jax import lax

HEADS = 16
HEAD = 128
FF = 8192
EXPERTS = 32
EXPF = 2
TOPK = 2
USERS = 4
BEAMS = 32
SEQ_DEV = 8
D = 2048
LEN = 256
ROWS = 1024
CAP = 16
N_DEV = 32


def draw_queries(key, part):
    key = jax.random.fold_in(key, 1)
    base = jnp.clip(jax.random.normal(key, (ROWS, D), jnp.float32), -9.0, 9.0)
    return base.astype(jnp.bfloat16)


def draw_keys(key, part):
    key = jax.random.fold_in(key, 2)
    base = jnp.clip(jax.random.normal(key, (USERS, LEN, D), jnp.float32), -9.0, 9.0)
    return base.astype(jnp.bfloat16)


def draw_beam_user(key, part):
    key = jax.random.fold_in(key, 4)
    order = jax.random.permutation(key, N_DEV)
    return (order % USERS).astype(jnp.int32)


def draw_routes(key, part):
    key = jax.random.fold_in(key, 3)
    key_full, key_count, key_perm, key_first, key_second, key_flip = jax.random.split(key, 6)
    full_expert = jax.random.randint(key_full, (), 0, EXPF)
    counts = jax.random.randint(key_count, (N_DEV, EXPF), 0, CAP + 1)
    counts = jnp.where(jnp.arange(EXPF)[None, :] == full_expert, CAP, counts)
    starts = jnp.cumsum(counts, axis=1) - counts
    orders = jax.vmap(lambda sub: jax.random.permutation(sub, BEAMS))(jax.random.split(key_perm, N_DEV))
    ranks = jnp.argsort(orders, axis=1).astype(jnp.int32)
    first = jax.random.randint(key_first, (N_DEV, BEAMS), EXPF, EXPERTS)
    for expert in range(EXPF):
        lower = starts[:, expert][:, None]
        upper = lower + counts[:, expert][:, None]
        first = jnp.where((ranks >= lower) & (ranks < upper), expert, first)
    other = jax.random.randint(key_second, (N_DEV, BEAMS), EXPF, EXPERTS - 1)
    second = jnp.where(other >= first, other + 1, other)
    flip = jax.random.randint(key_flip, (N_DEV, BEAMS), 0, 2)
    col_a = jnp.where(flip == 1, second, first)
    col_b = jnp.where(flip == 1, first, second)
    return jnp.stack([col_a, col_b], axis=-1).reshape(ROWS, TOPK).astype(jnp.int32)


def block_levels(key, extent, cuts, least, largest):
    def one(axis_at, shards_of):
        heights = jax.random.uniform(jax.random.fold_in(jax.random.fold_in(key, 6), axis_at), (shards_of,), jnp.float32, least / len(cuts), largest / len(cuts))
        return jnp.repeat(jnp.exp(heights), extent[axis_at] // shards_of).reshape((-1,) + (1,) * (len(extent) - axis_at - 1))

    factor_of = one(*cuts[0])
    for cut in cuts[1:]:
        factor_of = factor_of * one(*cut)
    return factor_of


def length_profile(amount, total, limit, lean):
    portions = [(1 << 20) // math.isqrt(grade ** lean) + 1 for grade in range(2, amount + 1)]
    rest, given = total - limit - (amount - 1), [1] * (amount - 1)
    while rest > 0:
        movable = [i for i in range(amount - 1) if given[i] < limit]
        whole, remaining = sum([portions[i] for i in movable]), rest
        for i in movable:
            more = min(limit - given[i], max(1, remaining * portions[i] // whole), rest)
            given[i] = given[i] + more
            rest = rest - more
    return np.array([limit] + given)


def ragged_sizes(own_key, number_of, total, most, skew):
    if number_of == 2:
        one = jax.random.randint(own_key, (), max(1, total - most), min(most, total - 1) + 1)
        return jnp.stack([one, total - one])
    sizes = jnp.asarray(length_profile(number_of, total, most, skew), jnp.int32)
    couples = (number_of - 1) // 2
    donor, receiver = sizes[1:1 + 2 * couples:2], sizes[2:2 + 2 * couples:2]
    margin = jnp.minimum(donor - 1, most - receiver)
    shifted = jax.random.randint(jax.random.fold_in(own_key, 1), (couples,), 0, 1 << 20) % (margin + 1)
    sizes = sizes.at[1:1 + 2 * couples:2].set(donor - shifted).at[2:2 + 2 * couples:2].set(receiver + shifted)
    return sizes[jax.random.permutation(jax.random.fold_in(own_key, 2), number_of)]


def scatter_about(own_key, shape, deviation, limit, cuts=(), held_as=jnp.bfloat16):
    values = jax.random.normal(own_key, shape, jnp.float32) * deviation
    if len(cuts) > 0:
        values = block_levels(own_key, shape, cuts, -0.22, 0.18) * values
    return jnp.clip(values, min=-limit, max=limit).astype(held_as)


def setup_inputs(seed: int = 0, part: int = 0) -> dict:
    key_list = jax.random.split(jax.random.key(seed), 11)
    part_keys = jax.random.split(jax.random.fold_in(key_list[10], part), 11)
    queries = draw_queries(jax.random.fold_in(jax.random.fold_in(key_list[10], part), 71), part)
    keys = draw_keys(jax.random.fold_in(jax.random.fold_in(key_list[10], part), 71), part)
    values = scatter_about(part_keys[2], (USERS, LEN, D), 4.0, 24.0, ((1, 32),))
    kv_count = jax.vmap(lambda own: ragged_sizes(own, N_DEV, 3 * LEN // 4, SEQ_DEV, 2))(jax.random.split(part_keys[3], USERS)).reshape((USERS, N_DEV)).astype(jnp.int32)
    beam_user = draw_beam_user(jax.random.fold_in(jax.random.fold_in(key_list[10], part), 71), part)
    routes = draw_routes(jax.random.fold_in(jax.random.fold_in(key_list[10], part), 71), part)
    route_gate = jnp.clip(0.2 + 0.8 * jax.random.uniform(part_keys[6], (ROWS, TOPK), jnp.float32) ** block_levels(part_keys[6], (ROWS, TOPK), ((0, 32),), -0.2, 0.2), 0.2, 1.0)
    norm_gain = jnp.clip(1.0 + 0.18 * jax.random.normal(key_list[7], (D,), jnp.float32), 0.1, 1.9)
    w_up = scatter_about(key_list[8], (D, EXPF * FF), D ** -0.5, 0.125, ((1, 32),))
    w_down = scatter_about(key_list[9], (EXPF * FF, D), FF ** -0.5, 0.0625, ((0, 32),))
    return dict(queries=queries, keys=keys, values=values, kv_count=kv_count, beam_user=beam_user, routes=routes, route_gate=route_gate, norm_gain=norm_gain, w_up=w_up, w_down=w_down)


def reference(queries, keys, values, kv_count, beam_user, routes, route_gate, norm_gain, w_up, w_down):
    scale = HEAD ** (-0.5)
    offset = jnp.arange(LEN) % SEQ_DEV
    shard = jnp.arange(LEN) // SEQ_DEV

    def attend(block):
        user = beam_user[block]
        start = (block * BEAMS).astype(jnp.int32)
        query_rows = lax.dynamic_slice_in_dim(queries, start, BEAMS, 0).astype(jnp.float32).reshape(BEAMS, HEADS, HEAD)
        user_keys = keys[user].astype(jnp.float32).reshape(LEN, HEADS, HEAD)
        user_values = values[user].astype(jnp.float32).reshape(LEN, HEADS, HEAD)
        valid = offset < kv_count[user][shard]
        scores = jnp.einsum('bhd,lhd->hbl', query_rows, user_keys) * scale
        scores = jnp.where(valid[None, None, :], scores, -1e+30)
        top = lax.optimization_barrier(jnp.max(scores, axis=-1, keepdims=True))
        expo = jnp.exp(scores - top)
        total = lax.optimization_barrier(jnp.sum(expo, axis=-1, keepdims=True))
        weights = lax.optimization_barrier((expo / total).astype(jnp.bfloat16)).astype(jnp.float32)
        mixed = jnp.einsum('hbl,lhd->bhd', weights, user_values)
        return mixed.reshape(BEAMS, D).astype(jnp.bfloat16)
    context = lax.map(attend, jnp.arange(N_DEV, dtype=jnp.int32)).reshape(ROWS, D)
    rows_f = queries.astype(jnp.float32)
    mean_sq = lax.optimization_barrier(jnp.mean(rows_f * rows_f, axis=-1, keepdims=True))
    normed = (rows_f * lax.rsqrt(mean_sq + 1e-06) * norm_gain[None, :]).astype(jnp.bfloat16)
    routed = jnp.zeros((ROWS, D), jnp.float32)
    for expert in range(EXPF):
        up_part = w_up[:, expert * FF:(expert + 1) * FF]
        down_part = w_down[expert * FF:(expert + 1) * FF]
        hidden = jax.nn.silu(jnp.dot(normed, up_part, preferred_element_type=jnp.float32)).astype(jnp.bfloat16)
        output = jnp.dot(hidden, down_part, preferred_element_type=jnp.float32)
        weight = lax.optimization_barrier(jnp.sum(jnp.where(routes == expert, route_gate, jnp.zeros_like(route_gate)), axis=1))
        routed = routed + weight[:, None] * output
    return (context, routed.astype(jnp.bfloat16))
```

```python
import functools

import jax
import jax.numpy as jnp
from jax import lax
from jax.experimental import pallas as pl
from jax.experimental.pallas import tpu as pltpu
from jax.sharding import PartitionSpec as P

HEAD = 128
EXPF = 2
CAP = 16
NX = 4
NZ = 8
HALF = NZ // EXPF
BF = jnp.bfloat16
F32 = jnp.float32

Z_RINGS = [[z * NX + x for z in range(NZ)] for x in range(NX)]
RIGHT = [(z * NX + x, z * NX + (x + 1) % NX) for z in range(NZ) for x in range(NX)]
LEFT = [(z * NX + x, z * NX + (x - 1) % NX) for z in range(NZ) for x in range(NX)]


def to_right(a):
    return lax.ppermute(a, "dev", RIGHT)


def to_left(a):
    return lax.ppermute(a, "dev", LEFT)


def along_z(a):
    return lax.all_to_all(
        a, "dev", split_axis=0, concat_axis=0, axis_index_groups=Z_RINGS, tiled=True
    )


def slot_columns(routes, expert):
    beams = routes.shape[0]
    chosen = jnp.sum((routes == expert).astype(F32), axis=1, keepdims=True)
    row = lax.broadcasted_iota(jnp.int32, (beams, beams), 0)
    col = lax.broadcasted_iota(jnp.int32, (beams, beams), 1)
    return chosen, row, col


def pack_rows_kernel(queries_ref, routes_ref, gain_ref, out_ref):
    rows = queries_ref[...].astype(F32)
    mean_sq = jnp.mean(rows * rows, axis=-1, keepdims=True)
    normed = (rows * lax.rsqrt(mean_sq + 1e-06) * gain_ref[...]).astype(BF)
    routes = routes_ref[...]
    beams = rows.shape[0]
    for expert in range(EXPF):
        chosen, row, col = slot_columns(routes, expert)
        slot = jnp.sum(jnp.where(row < col, chosen, 0.0), axis=0, keepdims=True)
        mine = jnp.sum(jnp.where(row == col, chosen, 0.0), axis=0, keepdims=True)
        place = lax.broadcasted_iota(jnp.int32, (CAP, beams), 0).astype(F32)
        picker = jnp.where((place == slot) & (mine > 0.5), 1.0, 0.0).astype(BF)
        packed = jnp.dot(picker, normed, preferred_element_type=F32).astype(BF)
        for z in range(HALF):
            out_ref[expert * HALF + z] = packed


def pack_rows(queries, routes, gain):
    width = queries.shape[1]
    return pl.pallas_call(
        pack_rows_kernel,
        out_shape=jax.ShapeDtypeStruct((NZ, CAP, width), BF),
        cost_estimate=pl.CostEstimate(
            flops=4_000_000, bytes_accessed=700_000, transcendentals=32
        ),
        name="pack_rows",
    )(queries, routes, gain.reshape(1, width))


def combine_kernel(ret_ref, routes_ref, gate_ref, out_ref):
    routes = routes_ref[...]
    gate = gate_ref[...]
    beams = routes.shape[0]
    total = None
    for expert in range(EXPF):
        summed = ret_ref[expert * HALF].astype(F32)
        for z in range(1, HALF):
            summed = summed + ret_ref[expert * HALF + z].astype(F32)
        chosen, row, col = slot_columns(routes, expert)
        mine = jnp.sum(jnp.where(row == col, chosen, 0.0), axis=0, keepdims=True)
        slot = jnp.sum(jnp.where(col < row, mine, 0.0), axis=1, keepdims=True)
        weight = jnp.sum(jnp.where(routes == expert, gate, 0.0), axis=1, keepdims=True)
        place = lax.broadcasted_iota(jnp.int32, (beams, CAP), 1).astype(F32)
        spread = jnp.where((place == slot) & (chosen > 0.5), weight, 0.0)
        part = jnp.dot(
            spread, summed, precision=lax.Precision.HIGHEST, preferred_element_type=F32
        )
        total = part if total is None else total + part
    out_ref[...] = total.astype(BF)


def combine(ret, routes, gate):
    beams = routes.shape[0]
    width = ret.shape[-1]
    return pl.pallas_call(
        combine_kernel,
        out_shape=jax.ShapeDtypeStruct((beams, width), BF),
        cost_estimate=pl.CostEstimate(
            flops=25_000_000, bytes_accessed=700_000, transcendentals=0
        ),
        name="combine",
    )(ret, routes, gate)


def pack_heads_kernel(q_ref, own_ref, left_ref, right_ref, kfar_ref, vfar_ref, out_ref):
    rows = q_ref.shape[0]
    shard = kfar_ref.shape[0]
    span = out_ref.shape[2]
    for z in range(NZ):
        cols = slice(z * span, (z + 1) * span)
        at = 0
        for which, far in ((0, kfar_ref), (1, vfar_ref)):
            for ref in (own_ref, left_ref, right_ref):
                out_ref[z, at : at + shard, :] = ref[which, :, cols]
                at += shard
            out_ref[z, at : at + shard, :] = far[:, cols]
            at += shard
        out_ref[z, at : at + rows, :] = q_ref[:, cols]


def pack_heads(queries, own, left, right, k_far, v_far):
    rows, width = queries.shape
    shard = k_far.shape[0]
    return pl.pallas_call(
        pack_heads_kernel,
        out_shape=jax.ShapeDtypeStruct((NZ, 2 * NX * shard + rows, width // NZ), BF),
        cost_estimate=pl.CostEstimate(
            flops=0, bytes_accessed=2_400_000, transcendentals=0
        ),
        name="pack_heads",
    )(queries, own, left, right, k_far, v_far)


def attend_kernel(beams, got_ref, bias_ref, out_ref):
    span = got_ref.shape[2]
    memory = (got_ref.shape[1] - beams) // 2
    count = NZ * memory
    for head in range(span // HEAD):
        cols = slice(head * HEAD, (head + 1) * HEAD)
        keys = got_ref[:, 0:memory, cols].reshape(count, HEAD)
        values = got_ref[:, memory : 2 * memory, cols].reshape(count, HEAD)
        for src in range(0, NZ, 2):
            rows = got_ref[src : src + 2, 2 * memory : 2 * memory + beams, cols]
            rows = rows.reshape(2 * beams, HEAD)
            scores = lax.dot_general(
                rows, keys, (((1,), (1,)), ((), ())), preferred_element_type=F32
            )
            scores = scores * HEAD ** (-0.5)
            scores = scores.reshape(2, beams, count) + bias_ref[src : src + 2][:, None, :]
            top = jnp.max(scores, axis=-1, keepdims=True)
            expo = jnp.exp(scores - top)
            total = jnp.sum(expo, axis=-1, keepdims=True)
            weights = (expo / total).astype(BF).reshape(2 * beams, count)
            mixed = jnp.dot(weights, values, preferred_element_type=F32).astype(BF)
            out_ref[src : src + 2, :, cols] = mixed.reshape(2, beams, HEAD)


def attend(got, bias, beams):
    span = got.shape[2]
    return pl.pallas_call(
        functools.partial(attend_kernel, beams),
        out_shape=jax.ShapeDtypeStruct((NZ, beams, span), BF),
        cost_estimate=pl.CostEstimate(
            flops=300_000_000, bytes_accessed=1_400_000, transcendentals=600_000
        ),
        compiler_params=pltpu.CompilerParams(vmem_limit_bytes=24 * 2**20),
        name="attend",
    )(got, bias)


def experts_kernel(count, *refs):
    ins, (up_ref, down_ref), outs = refs[:count], refs[count : count + 2], refs[count + 2 : -1]
    acc = refs[-1]
    step = pl.program_id(0)
    at = 0
    for rows_ref in ins:
        size = rows_ref.shape[0]
        hidden = jnp.dot(rows_ref[...], up_ref[...], preferred_element_type=F32)
        hidden = (hidden / (1.0 + jnp.exp(-hidden))).astype(BF)
        part = jnp.dot(hidden, down_ref[...], preferred_element_type=F32)
        span = slice(at, at + size)

        @pl.when(step == 0)
        def _(part=part, span=span):
            acc[span, :] = part

        @pl.when(step != 0)
        def _(part=part, span=span):
            acc[span, :] += part

        at += size

    @pl.when(step == pl.num_programs(0) - 1)
    def _():
        at = 0
        for out_ref in outs:
            size = out_ref.shape[0]
            out_ref[...] = acc[at : at + size, :].astype(out_ref.dtype)
            at += size


def experts(blocks, up, down, tile=256):
    width, hidden = up.shape
    total = sum(b.shape[0] for b in blocks)
    whole = [pl.BlockSpec(b.shape, lambda j: (0, 0)) for b in blocks]
    return pl.pallas_call(
        functools.partial(experts_kernel, len(blocks)),
        grid=(hidden // tile,),
        in_specs=whole
        + [
            pl.BlockSpec((width, tile), lambda j: (0, j)),
            pl.BlockSpec((tile, width), lambda j: (j, 0)),
        ],
        out_specs=list(whole),
        out_shape=[jax.ShapeDtypeStruct(b.shape, BF) for b in blocks],
        scratch_shapes=[pltpu.VMEM((total, width), F32)],
        cost_estimate=pl.CostEstimate(
            flops=4 * total * width * hidden,
            bytes_accessed=4 * width * hidden + 4 * total * width,
            transcendentals=total * hidden,
        ),
        compiler_params=pltpu.CompilerParams(vmem_limit_bytes=32 * 2**20),
        name="experts",
    )(*blocks, up, down)


def on_device(
    queries, keys, values, kv_count, beam_user, routes, route_gate, norm_gain, w_up, w_down
):
    beams, width = queries.shape
    users, shard_len, _ = keys.shape
    shard = users * shard_len
    x = lax.rem(lax.axis_index("dev"), NX)

    own = jnp.stack([keys.reshape(shard, width), values.reshape(shard, width)])
    left, right = to_right(own), to_left(own)
    k_far, v_far = to_right(left[0]), to_left(right[1])

    block = along_z(pack_rows(queries, routes, norm_gain))
    size = NZ * CAP
    block = block.reshape(size, width)
    block_l, block_r = to_right(block), to_left(block)
    far_a, far_b = to_right(block_l[: size // 2]), to_left(block_r[size // 2 :])

    (part,) = experts([block], w_up, w_down)
    part_l, part_r = experts([block_l, block_r], w_up, w_down)
    part_fa, part_fb = experts([far_a, far_b], w_up, w_down)

    got = along_z(pack_heads(queries, own, left, right, k_far, v_far))
    order = jnp.stack([x, lax.rem(x + NX - 1, NX), lax.rem(x + 1, NX), lax.rem(x + 2, NX)])
    counts = jnp.take(kv_count.reshape(users, NZ, NX), order, axis=2)
    counts = counts.transpose(1, 2, 0)[None, :, :, :, None]
    column_users = beam_user.reshape(NZ, NX)[:, x]
    offset = jnp.arange(shard_len)[None, None, None, None, :]
    same = column_users[:, None, None, None, None] == jnp.arange(users)[None, None, None, :, None]
    bias = jnp.where(same & (offset < counts), 0.0, -1e30).astype(F32)
    mixed = along_z(attend(got, bias.reshape(NZ, NZ * NX * shard), beams))
    context = mixed.transpose(1, 0, 2).reshape(beams, width)

    half = size // 2
    more_r = to_right(part_fa)
    more_l = to_left(part_fb)
    part_r = jnp.concatenate(
        [(part_r[:half].astype(F32) + more_r.astype(F32)).astype(BF), part_r[half:]]
    )
    part_l = jnp.concatenate(
        [part_l[:half], (part_l[half:].astype(F32) + more_l.astype(F32)).astype(BF)]
    )
    from_l, from_r = to_right(part_r), to_left(part_l)
    total = (part.astype(F32) + from_l.astype(F32) + from_r.astype(F32)).astype(BF)
    ret = along_z(total.reshape(NZ, CAP, width))
    routed = combine(ret, routes, route_gate)
    return (context, routed)


def solution(mesh):
    return jax.shard_map(
        on_device,
        mesh=mesh,
        in_specs=(
            P(("user", "dev"), None),
            P("user", "dev", None),
            P("user", "dev", None),
            P("user", None),
            P("user"),
            P(("user", "dev"), None),
            P(("user", "dev"), None),
            P(),
            P(None, "dev"),
            P("dev", None),
        ),
        out_specs=(P(("user", "dev"), None), P(("user", "dev"), None)),
        check_vma=False,
    )
```

```python
import functools

import jax
import jax.numpy as jnp
from jax import lax
from jax.experimental import pallas as pl
from jax.experimental.pallas import tpu as pltpu
from jax.sharding import PartitionSpec as P

HEAD = 128
EXPF = 2
CAP = 16
NX = 4
NZ = 8
HALF = NZ // EXPF
BF = jnp.bfloat16
F32 = jnp.float32

Z_RINGS = [[z * NX + x for z in range(NZ)] for x in range(NX)]
RIGHT = [(z * NX + x, z * NX + (x + 1) % NX) for z in range(NZ) for x in range(NX)]
FAR = [(z * NX + x, z * NX + (x + 2) % NX) for z in range(NZ) for x in range(NX)]
LEFT = [(z * NX + x, z * NX + (x - 1) % NX) for z in range(NZ) for x in range(NX)]


def to_right(a):
    return lax.ppermute(a, "dev", RIGHT)


def to_left(a):
    return lax.ppermute(a, "dev", LEFT)


def to_far(a):
    return lax.ppermute(a, "dev", FAR)


def along_z(a):
    return lax.all_to_all(
        a, "dev", split_axis=0, concat_axis=0, axis_index_groups=Z_RINGS, tiled=True
    )


def in_hbm(*arrays):
    return [pltpu.with_memory_space_constraint(a, pltpu.HBM) for a in arrays]


def turn(row):
    n = row.shape[1]
    at = lax.broadcasted_iota(jnp.int32, (n, n), 0)
    to = lax.broadcasted_iota(jnp.int32, (n, n), 1)
    return jnp.sum(jnp.where(at == to, row, 0.0), axis=1, keepdims=True)


def pack_rows_kernel(
    queries_ref, routes_ref, gain_ref, keys_ref, values_ref, out_ref, both_ref, sems
):
    copies = [
        pltpu.make_async_copy(ref, both_ref.at[at], sems.at[at])
        for at, ref in enumerate((keys_ref, values_ref))
    ]
    for copy in copies:
        copy.start()
    rows = queries_ref[...].astype(F32)
    mean_sq = jnp.mean(rows * rows, axis=-1, keepdims=True)
    normed = (rows * lax.rsqrt(mean_sq + 1e-06) * gain_ref[...]).astype(BF)
    routes = routes_ref[...]
    beams = rows.shape[0]
    at = lax.broadcasted_iota(jnp.int32, (beams, beams), 0)
    to = lax.broadcasted_iota(jnp.int32, (beams, beams), 1)
    place = lax.broadcasted_iota(jnp.int32, (CAP, beams), 0).astype(F32)
    for expert in range(EXPF):
        mine = jnp.sum((routes == expert).astype(F32), axis=0, keepdims=True)
        slot = jnp.sum(jnp.where(at < to, turn(mine), 0.0), axis=0, keepdims=True)
        picker = jnp.where((place == slot) & (mine > 0.5), 1.0, 0.0).astype(BF)
        packed = jnp.dot(picker, normed, preferred_element_type=F32).astype(BF)
        for z in range(HALF):
            out_ref[expert * HALF + z] = packed
    for copy in copies:
        copy.wait()


def pack_rows(queries, routes, gain, keys, values):
    width = queries.shape[1]
    args = (queries, routes, gain.reshape(1, width), keys, values)
    args = in_hbm(*args)
    return pl.pallas_call(
        pack_rows_kernel,
        in_specs=[pl.BlockSpec(memory_space=pltpu.VMEM)] * 3
        + [pl.BlockSpec(memory_space=pl.ANY)] * 2,
        out_specs=[
            pl.BlockSpec(memory_space=pltpu.VMEM),
            pl.BlockSpec(memory_space=pl.ANY),
        ],
        out_shape=[
            jax.ShapeDtypeStruct((NZ, CAP, width), BF),
            jax.ShapeDtypeStruct((2, *keys.shape), BF),
        ],
        scratch_shapes=[pltpu.SemaphoreType.DMA((2,))],
        cost_estimate=pl.CostEstimate(
            flops=4_000_000, bytes_accessed=1_200_000, transcendentals=32
        ),
        compiler_params=pltpu.CompilerParams(vmem_limit_bytes=4 * 2**20),
        name="pack_rows",
    )(*args)


def finish_kernel(own_ref, left_ref, right_ref, far_ref, mixed_ref, out_ref):
    span = out_ref.shape[2]
    pieces = own_ref.shape[1] // span
    for piece in range(pieces):
        cols = slice(piece * span, (piece + 1) * span)
        total = own_ref[:, cols].astype(F32) + left_ref[:, cols].astype(F32)
        total = total + right_ref[:, cols].astype(F32) + far_ref[:, cols].astype(F32)
        out_ref[:, piece * CAP : (piece + 1) * CAP, :] = total.astype(BF).reshape(NZ, CAP, span)
    out_ref[:, pieces * CAP :, :] = mixed_ref[...]


def finish(own, left, right, far, mixed):
    beams, span = mixed.shape[1:]
    pieces = own.shape[1] // span
    return pl.pallas_call(
        finish_kernel,
        out_shape=jax.ShapeDtypeStruct((NZ, pieces * CAP + beams, span), BF),
        cost_estimate=pl.CostEstimate(
            flops=1_000_000, bytes_accessed=2_900_000, transcendentals=0
        ),
        compiler_params=pltpu.CompilerParams(vmem_limit_bytes=8 * 2**20),
        name="finish",
    )(own, left, right, far, mixed)


def combine_kernel(ret_ref, routes_ref, gate_ref, context_ref, routed_ref):
    routes = routes_ref[...]
    gate = gate_ref[...]
    beams = routes.shape[1]
    span = ret_ref.shape[2]
    pieces = routed_ref.shape[1] // span
    at = lax.broadcasted_iota(jnp.int32, (beams, beams), 0)
    to = lax.broadcasted_iota(jnp.int32, (beams, beams), 1)
    place = lax.broadcasted_iota(jnp.int32, (beams, CAP), 1).astype(F32)
    spread = []
    for expert in range(EXPF):
        mine = jnp.sum((routes == expert).astype(F32), axis=0, keepdims=True)
        slot = jnp.sum(jnp.where(to < at, mine, 0.0), axis=1, keepdims=True)
        weight = jnp.sum(jnp.where(routes == expert, gate, 0.0), axis=0, keepdims=True)
        spread.append(jnp.where((place == slot) & (turn(mine) > 0.5), turn(weight), 0.0))
    for piece in range(pieces):
        rows = slice(piece * CAP, (piece + 1) * CAP)
        total = None
        for expert in range(EXPF):
            summed = ret_ref[expert * HALF, rows, :].astype(F32)
            for z in range(1, HALF):
                summed = summed + ret_ref[expert * HALF + z, rows, :].astype(F32)
            part = jnp.dot(
                spread[expert],
                summed,
                precision=lax.Precision.HIGHEST,
                preferred_element_type=F32,
            )
            total = part if total is None else total + part
        routed_ref[:, piece * span : (piece + 1) * span] = total.astype(BF)
    for z in range(NZ):
        context_ref[:, z * span : (z + 1) * span] = ret_ref[z, pieces * CAP :, :]


def combine(ret, routes, gate, beams, width):
    shape = jax.ShapeDtypeStruct((beams, width), BF)
    return pl.pallas_call(
        combine_kernel,
        out_shape=[shape, shape],
        cost_estimate=pl.CostEstimate(
            flops=25_000_000, bytes_accessed=1_000_000, transcendentals=0
        ),
        compiler_params=pltpu.CompilerParams(vmem_limit_bytes=6 * 2**20),
        name="combine",
    )(ret, routes, gate)


def pack_heads_kernel(q_ref, own_ref, left_ref, right_ref, far_ref, out_ref):
    rows = q_ref.shape[0]
    shard = own_ref.shape[1]
    span = out_ref.shape[2]
    for z in range(NZ):
        cols = slice(z * span, (z + 1) * span)
        at = 0
        for which in (0, 1):
            for ref in (own_ref, left_ref, right_ref, far_ref):
                out_ref[z, at : at + shard, :] = ref[which, :, cols]
                at += shard
        out_ref[z, at : at + rows, :] = q_ref[:, cols]


def pack_heads(queries, own, left, right, far):
    rows, width = queries.shape
    shard = own.shape[1]
    return pl.pallas_call(
        pack_heads_kernel,
        out_shape=jax.ShapeDtypeStruct((NZ, 2 * NX * shard + rows, width // NZ), BF),
        cost_estimate=pl.CostEstimate(
            flops=20_000_000_000, bytes_accessed=2_400_000, transcendentals=0
        ),
        compiler_params=pltpu.CompilerParams(vmem_limit_bytes=8 * 2**20),
        name="pack_heads",
    )(queries, own, left, right, far)


def valid_positions(counts, shard):
    users, shards = counts.shape
    offsets = shard // users
    total = shards * shard
    at = lax.broadcasted_iota(jnp.int32, (shards, total), 1)
    shard_of = at // shard
    step = shard_of % NX
    step = jnp.where(step == 1, NX - 1, jnp.where(step == 2, 1, jnp.where(step == 3, 2, 0)))
    x = (lax.axis_index("dev") + step) % NX
    source = shard_of // NX * NX + x
    spread = (source == lax.broadcasted_iota(jnp.int32, (shards, total), 0)).astype(F32)
    found = jnp.dot(counts.astype(F32), spread, preferred_element_type=F32)
    at = at[:users]
    user = at // offsets % users
    mine = user == lax.broadcasted_iota(jnp.int32, (users, total), 0)
    limit = jnp.sum(jnp.where(mine, found, 0.0), axis=0, keepdims=True)
    return user[:1], (at[:1] % offsets).astype(F32) < limit - 0.5


def attend_kernel(owner_ref, got_ref, counts_ref, out_ref, *, beams, group):
    span = got_ref.shape[2]
    memory = (got_ref.shape[1] - beams) // 2
    count = NZ * memory
    user, valid = valid_positions(counts_ref[...], memory // NX)
    x = lax.axis_index("dev") % NX
    biases = []
    for src in range(NZ):
        mine = user == owner_ref[src * NX + x]
        biases.append(jnp.where(mine & valid, 0.0, -1e30))
    for head in range(span // HEAD):
        cols = slice(head * HEAD, (head + 1) * HEAD)
        keys = got_ref[:, 0:memory, cols].reshape(count, HEAD)
        values = got_ref[:, memory : 2 * memory, cols].reshape(count, HEAD)
        for src in range(0, NZ, group):
            own = slice(src, src + group)
            rows = got_ref[own, 2 * memory : 2 * memory + beams, cols]
            rows = rows.reshape(group * beams, HEAD)
            scores = lax.dot_general(
                rows, keys, (((1,), (1,)), ((), ())), preferred_element_type=F32
            )
            scores = jnp.concatenate(
                [
                    scores[at * beams : (at + 1) * beams] * HEAD ** (-0.5) + biases[src + at]
                    for at in range(group)
                ],
                axis=0,
            )
            top = jnp.max(scores, axis=-1, keepdims=True)
            expo = jnp.exp(scores - top)
            total = jnp.sum(expo, axis=-1, keepdims=True)
            weights = (expo * (1.0 / total)).astype(BF)
            mixed = jnp.dot(weights, values, preferred_element_type=F32).astype(BF)
            out_ref[own, :, cols] = mixed.reshape(group, beams, HEAD)


def attend(got, counts, owner, beams):
    span = got.shape[2]
    return pl.pallas_call(
        functools.partial(attend_kernel, beams=beams, group=2),
        in_specs=[
            pl.BlockSpec(memory_space=pltpu.SMEM),
            pl.BlockSpec(memory_space=pltpu.VMEM),
            pl.BlockSpec(memory_space=pltpu.VMEM),
        ],
        out_shape=jax.ShapeDtypeStruct((NZ, beams, span), BF),
        cost_estimate=pl.CostEstimate(
            flops=300_000_000, bytes_accessed=1_400_000, transcendentals=600_000
        ),
        compiler_params=pltpu.CompilerParams(vmem_limit_bytes=12 * 2**20),
        name="attend",
    )(owner, got, *in_hbm(counts))


def experts_kernel(rows_ref, up_ref, down_ref, out_ref, up, down, sems):
    copies = []
    for which, (source, target) in enumerate(((up_ref, up), (down_ref, down))):
        size = target.shape[0] // 2
        for half in range(2):
            own = slice(half * size, (half + 1) * size)
            copies.append(
                pltpu.make_async_copy(source.at[own], target.at[own], sems.at[which, half])
            )
            copies[-1].start()
    value = rows_ref[...]
    for which, weight in enumerate((up, down)):
        size = weight.shape[0] // 2
        total = None
        for half in range(2):
            own = slice(half * size, (half + 1) * size)
            copies[which * 2 + half].wait()
            part = jnp.dot(value[:, own], weight[own, :], preferred_element_type=F32)
            total = part if total is None else total + part
        if which == 0:
            value = (total / (1.0 + jnp.exp(-total))).astype(BF)
    out_ref[...] = total.astype(BF)


def experts(rows, up, down):
    size = rows.shape[0]
    width, hidden = up.shape
    return pl.pallas_call(
        experts_kernel,
        in_specs=[pl.BlockSpec(memory_space=pltpu.VMEM)]
        + [pl.BlockSpec(memory_space=pl.ANY)] * 2,
        out_shape=jax.ShapeDtypeStruct(rows.shape, BF),
        scratch_shapes=[
            pltpu.VMEM(up.shape, up.dtype),
            pltpu.VMEM(down.shape, down.dtype),
            pltpu.SemaphoreType.DMA((2, 2)),
        ],
        cost_estimate=pl.CostEstimate(
            flops=400 * size * width * hidden,
            bytes_accessed=4 * width * hidden + 4 * size * width,
            transcendentals=size * hidden,
        ),
        compiler_params=pltpu.CompilerParams(vmem_limit_bytes=10 * 2**20),
        name="experts",
    )(rows, *in_hbm(up, down))


def on_device(
    queries, keys, values, kv_count, beam_user, routes, route_gate, norm_gain, w_up, w_down
):
    beams, width = queries.shape
    users, shard_len, _ = keys.shape
    shard = users * shard_len
    x = lax.rem(lax.axis_index("dev"), NX)

    routes, route_gate = routes.T, route_gate.T

    size = NZ * CAP
    packed, own = pack_rows(
        queries, routes, norm_gain, keys.reshape(shard, width), values.reshape(shard, width)
    )
    left, right, far = to_right(own), to_left(own), to_far(own)
    block = along_z(packed).reshape(size, width)
    block, far = lax.optimization_barrier((block, far))
    block_f, block_l, block_r = to_far(block), to_right(block), to_left(block)
    part = experts(block, w_up, w_down)

    got = along_z(pack_heads(queries, own, left, right, far))
    mixed = attend(got, kv_count, beam_user, beams)

    part_l = experts(block_l, w_up, w_down)
    from_r = to_left(part_l)
    part_r = experts(block_r, w_up, w_down)
    from_l = to_right(part_r)
    part_f = experts(block_f, w_up, w_down)
    from_f = to_far(part_f)
    ret = along_z(finish(part, from_l, from_r, from_f, mixed))
    context, routed = combine(ret, routes, route_gate, beams, width)
    return (context, routed)


def solution(mesh):
    return jax.shard_map(
        on_device,
        mesh=mesh,
        in_specs=(
            P(("user", "dev"), None),
            P("user", "dev", None),
            P("user", "dev", None),
            P("user", None),
            P("user"),
            P(("user", "dev"), None),
            P(("user", "dev"), None),
            P(),
            P(None, "dev"),
            P("dev", None),
        ),
        out_specs=(P(("user", "dev"), None), P(("user", "dev"), None)),
        check_vma=False,
    )
```

```python
import functools

import jax
import jax.numpy as jnp
from jax import lax
from jax.experimental import pallas as pl
from jax.experimental.pallas import tpu as pltpu
from jax.sharding import PartitionSpec as P

HEAD = 128
EXPF = 2
CAP = 16
NX = 4
NZ = 8
HALF = NZ // EXPF
BF = jnp.bfloat16
F32 = jnp.float32

FIRST = list(range(NZ))
LAST = list(range(NZ))[::-1]
RIGHT = [(z * NX + x, z * NX + (x + 1) % NX) for z in range(NZ) for x in range(NX)]
FAR = [(z * NX + x, z * NX + (x + 2) % NX) for z in range(NZ) for x in range(NX)]
LEFT = [(z * NX + x, z * NX + (x - 1) % NX) for z in range(NZ) for x in range(NX)]


def to_right(a):
    return lax.ppermute(a, "dev", RIGHT)


def to_left(a):
    return lax.ppermute(a, "dev", LEFT)


def to_far(a):
    return lax.ppermute(a, "dev", FAR)


def along_z(a, order=tuple(range(NZ))):
    rings = [[z * NX + x for z in order] for x in range(NX)]
    return lax.all_to_all(
        a, "dev", split_axis=0, concat_axis=0, axis_index_groups=rings, tiled=True
    )


def in_hbm(*arrays):
    return [pltpu.with_memory_space_constraint(a, pltpu.HBM) for a in arrays]


def turn(row):
    n = row.shape[1]
    at = lax.broadcasted_iota(jnp.int32, (n, n), 0)
    to = lax.broadcasted_iota(jnp.int32, (n, n), 1)
    return jnp.sum(jnp.where(at == to, row, 0.0), axis=1, keepdims=True)


def pack_rows_kernel(queries_ref, routes_ref, gain_ref, out_ref):
    rows = queries_ref[...].astype(F32)
    mean_sq = jnp.mean(rows * rows, axis=-1, keepdims=True)
    normed = (rows * lax.rsqrt(mean_sq + 1e-06) * gain_ref[...]).astype(BF)
    routes = routes_ref[...]
    beams = rows.shape[0]
    at = lax.broadcasted_iota(jnp.int32, (beams, beams), 0)
    to = lax.broadcasted_iota(jnp.int32, (beams, beams), 1)
    place = lax.broadcasted_iota(jnp.int32, (CAP, beams), 0).astype(F32)
    for expert in range(EXPF):
        mine = jnp.sum((routes == expert).astype(F32), axis=0, keepdims=True)
        slot = jnp.sum(jnp.where(at < to, turn(mine), 0.0), axis=0, keepdims=True)
        picker = jnp.where((place == slot) & (mine > 0.5), 1.0, 0.0).astype(BF)
        packed = jnp.dot(picker, normed, preferred_element_type=F32).astype(BF)
        for z in range(expert * HALF, (expert + 1) * HALF):
            out_ref[FIRST.index(z)] = packed


def pack_rows(queries, routes, gain):
    width = queries.shape[1]
    return pl.pallas_call(
        pack_rows_kernel,
        out_shape=jax.ShapeDtypeStruct((NZ, CAP, width), BF),
        cost_estimate=pl.CostEstimate(
            flops=4_000_000, bytes_accessed=700_000, transcendentals=32
        ),
        compiler_params=pltpu.CompilerParams(vmem_limit_bytes=4 * 2**20),
        name="pack_rows",
    )(*in_hbm(queries, routes, gain.reshape(1, width)))


def finish_kernel(own_ref, left_ref, right_ref, far_ref, mixed_ref, out_ref):
    span = out_ref.shape[2]
    pieces = own_ref.shape[1] // span
    for z in range(NZ):
        rows = slice(FIRST.index(z) * CAP, (FIRST.index(z) + 1) * CAP)
        place = LAST.index(z)
        total = own_ref[rows].astype(F32) + left_ref[rows].astype(F32)
        total = total + right_ref[rows].astype(F32) + far_ref[rows].astype(F32)
        total = total.astype(BF)
        for piece in range(pieces):
            cols = slice(piece * span, (piece + 1) * span)
            out_ref[place, piece * CAP : (piece + 1) * CAP, :] = total[:, cols]
        out_ref[place, pieces * CAP :, :] = mixed_ref[z]


def finish(own, left, right, far, mixed):
    beams, span = mixed.shape[1:]
    pieces = own.shape[1] // span
    return pl.pallas_call(
        finish_kernel,
        out_shape=jax.ShapeDtypeStruct((NZ, pieces * CAP + beams, span), BF),
        cost_estimate=pl.CostEstimate(
            flops=1_000_000, bytes_accessed=2_900_000, transcendentals=0
        ),
        compiler_params=pltpu.CompilerParams(vmem_limit_bytes=8 * 2**20),
        name="finish",
    )(own, left, right, far, mixed)


def combine_kernel(ret_ref, routes_ref, gate_ref, context_ref, routed_ref):
    routes = routes_ref[...]
    gate = gate_ref[...]
    beams = routes.shape[1]
    span = ret_ref.shape[2]
    pieces = routed_ref.shape[1] // span
    at = lax.broadcasted_iota(jnp.int32, (beams, beams), 0)
    to = lax.broadcasted_iota(jnp.int32, (beams, beams), 1)
    place = lax.broadcasted_iota(jnp.int32, (beams, CAP), 1).astype(F32)
    spread = []
    for expert in range(EXPF):
        mine = jnp.sum((routes == expert).astype(F32), axis=0, keepdims=True)
        slot = jnp.sum(jnp.where(to < at, mine, 0.0), axis=1, keepdims=True)
        weight = jnp.sum(jnp.where(routes == expert, gate, 0.0), axis=0, keepdims=True)
        spread.append(jnp.where((place == slot) & (turn(mine) > 0.5), turn(weight), 0.0))
    for piece in range(pieces):
        rows = slice(piece * CAP, (piece + 1) * CAP)
        total = None
        for expert in range(EXPF):
            summed = None
            for z in range(expert * HALF, (expert + 1) * HALF):
                term = ret_ref[LAST.index(z), rows, :].astype(F32)
                summed = term if summed is None else summed + term
            part = jnp.dot(
                spread[expert],
                summed,
                precision=lax.Precision.HIGHEST,
                preferred_element_type=F32,
            )
            total = part if total is None else total + part
        routed_ref[:, piece * span : (piece + 1) * span] = total.astype(BF)
    for z in range(NZ):
        context_ref[:, z * span : (z + 1) * span] = ret_ref[LAST.index(z), pieces * CAP :, :]


def combine(ret, routes, gate, beams, width):
    shape = jax.ShapeDtypeStruct((beams, width), BF)
    return pl.pallas_call(
        combine_kernel,
        out_shape=[shape, shape],
        cost_estimate=pl.CostEstimate(
            flops=25_000_000, bytes_accessed=1_000_000, transcendentals=0
        ),
        compiler_params=pltpu.CompilerParams(vmem_limit_bytes=6 * 2**20),
        name="combine",
    )(ret, routes, gate)


def pack_heads_kernel(q_ref, own_ref, left_ref, right_ref, far_ref, out_ref):
    rows = q_ref.shape[0]
    shard = own_ref.shape[1]
    span = out_ref.shape[2]
    for z in range(NZ):
        cols = slice(z * span, (z + 1) * span)
        at = 0
        for which in (0, 1):
            for ref in (own_ref, left_ref, right_ref, far_ref):
                out_ref[z, at : at + shard, :] = ref[which, :, cols]
                at += shard
        out_ref[z, at : at + rows, :] = q_ref[:, cols]


def pack_heads(queries, own, left, right, far):
    rows, width = queries.shape
    shard = own.shape[1]
    return pl.pallas_call(
        pack_heads_kernel,
        out_shape=jax.ShapeDtypeStruct((NZ, 2 * NX * shard + rows, width // NZ), BF),
        cost_estimate=pl.CostEstimate(
            flops=20_000_000_000, bytes_accessed=2_400_000, transcendentals=0
        ),
        compiler_params=pltpu.CompilerParams(vmem_limit_bytes=8 * 2**20),
        name="pack_heads",
    )(queries, own, left, right, far)


def valid_positions(counts, shard):
    users, shards = counts.shape
    offsets = shard // users
    total = shards * shard
    at = lax.broadcasted_iota(jnp.int32, (shards, total), 1)
    shard_of = at // shard
    step = shard_of % NX
    step = jnp.where(step == 1, NX - 1, jnp.where(step == 2, 1, jnp.where(step == 3, 2, 0)))
    x = (lax.axis_index("dev") + step) % NX
    source = shard_of // NX * NX + x
    spread = (source == lax.broadcasted_iota(jnp.int32, (shards, total), 0)).astype(F32)
    found = jnp.dot(counts.astype(F32), spread, preferred_element_type=F32)
    at = at[:users]
    user = at // offsets % users
    mine = user == lax.broadcasted_iota(jnp.int32, (users, total), 0)
    limit = jnp.sum(jnp.where(mine, found, 0.0), axis=0, keepdims=True)
    return user[:1], (at[:1] % offsets).astype(F32) < limit - 0.5


def attend_kernel(owner_ref, got_ref, counts_ref, out_ref, *, beams, group):
    span = got_ref.shape[2]
    memory = (got_ref.shape[1] - beams) // 2
    count = NZ * memory
    user, valid = valid_positions(counts_ref[...], memory // NX)
    x = lax.axis_index("dev") % NX
    biases = []
    for src in range(NZ):
        mine = user == owner_ref[src * NX + x]
        biases.append(jnp.where(mine & valid, 0.0, -1e30))
    for head in range(span // HEAD):
        cols = slice(head * HEAD, (head + 1) * HEAD)
        keys = got_ref[:, 0:memory, cols].reshape(count, HEAD)
        values = got_ref[:, memory : 2 * memory, cols].reshape(count, HEAD)
        for src in range(0, NZ, group):
            own = slice(src, src + group)
            rows = got_ref[own, 2 * memory : 2 * memory + beams, cols]
            rows = rows.reshape(group * beams, HEAD)
            scores = lax.dot_general(
                rows, keys, (((1,), (1,)), ((), ())), preferred_element_type=F32
            )
            scores = jnp.concatenate(
                [
                    scores[at * beams : (at + 1) * beams] * HEAD ** (-0.5) + biases[src + at]
                    for at in range(group)
                ],
                axis=0,
            )
            top = jnp.max(scores, axis=-1, keepdims=True)
            expo = jnp.exp(scores - top)
            total = jnp.sum(expo, axis=-1, keepdims=True)
            weights = (expo * (1.0 / total)).astype(BF)
            mixed = jnp.dot(weights, values, preferred_element_type=F32).astype(BF)
            out_ref[own, :, cols] = mixed.reshape(group, beams, HEAD)


def attend(got, counts, owner, beams):
    span = got.shape[2]
    return pl.pallas_call(
        functools.partial(attend_kernel, beams=beams, group=8),
        in_specs=[
            pl.BlockSpec(memory_space=pltpu.SMEM),
            pl.BlockSpec(memory_space=pltpu.VMEM),
            pl.BlockSpec(memory_space=pltpu.VMEM),
        ],
        out_shape=jax.ShapeDtypeStruct((NZ, beams, span), BF),
        cost_estimate=pl.CostEstimate(
            flops=300_000_000, bytes_accessed=1_400_000, transcendentals=600_000
        ),
        compiler_params=pltpu.CompilerParams(vmem_limit_bytes=12 * 2**20),
        name="attend",
    )(owner, got, *in_hbm(counts))


def experts_kernel(*refs):
    *ins, up_ref, down_ref = refs[: len(refs) // 2]
    *outs, up, down, sems = refs[len(refs) // 2 :]
    parts = 2
    copies = []
    for which, (source, target) in enumerate(((up_ref, up), (down_ref, down))):
        size = target.shape[0] // parts
        for part in range(parts):
            own = slice(part * size, (part + 1) * size)
            copies.append(
                pltpu.make_async_copy(source.at[own], target.at[own], sems.at[which, part])
            )
    ahead = 4
    for copy in copies[:ahead]:
        copy.start()
    value = jnp.concatenate([ref[...] for ref in ins], axis=0)
    for which, weight in enumerate((up, down)):
        size = weight.shape[0] // parts
        total = None
        for part in range(parts):
            own = slice(part * size, (part + 1) * size)
            index = which * parts + part
            copies[index].wait()
            if index + ahead < len(copies):
                copies[index + ahead].start()
            term = jnp.dot(value[:, own], weight[own, :], preferred_element_type=F32)
            total = term if total is None else total + term
        if which == 0:
            value = (total / (1.0 + jnp.exp(-total))).astype(BF)
    size = ins[0].shape[0]
    for index, out_ref in enumerate(outs):
        out_ref[...] = total[index * size : (index + 1) * size].astype(BF)


def experts(blocks, up, down):
    count = len(blocks)
    size = count * blocks[0].shape[0]
    width, hidden = up.shape
    return pl.pallas_call(
        experts_kernel,
        in_specs=[pl.BlockSpec(memory_space=pltpu.VMEM)] * count
        + [pl.BlockSpec(memory_space=pl.ANY)] * 2,
        out_shape=[jax.ShapeDtypeStruct(block.shape, BF) for block in blocks],
        scratch_shapes=[
            pltpu.VMEM(up.shape, up.dtype),
            pltpu.VMEM(down.shape, down.dtype),
            pltpu.SemaphoreType.DMA((2, 2)),
        ],
        cost_estimate=pl.CostEstimate(
            flops=400 * size * width * hidden,
            bytes_accessed=4 * width * hidden + 4 * size * width,
            transcendentals=size * hidden,
        ),
        compiler_params=pltpu.CompilerParams(vmem_limit_bytes=14 * 2**20),
        name="experts",
    )(*blocks, *in_hbm(up, down))


def on_device(
    queries, keys, values, kv_count, beam_user, routes, route_gate, norm_gain, w_up, w_down
):
    beams, width = queries.shape
    users, shard_len, _ = keys.shape
    shard = users * shard_len
    x = lax.rem(lax.axis_index("dev"), NX)

    routes, route_gate = routes.T, route_gate.T

    size = NZ * CAP
    packed = pack_rows(queries, routes, norm_gain)
    own = jnp.stack([keys.reshape(shard, width), values.reshape(shard, width)])
    left, right, far = to_right(own), to_left(own), to_far(own)
    block = along_z(packed, FIRST).reshape(size, width)
    block, far = lax.optimization_barrier((block, far))
    block_f, block_l, block_r = to_far(block), to_right(block), to_left(block)
    (part,) = experts([block], w_up, w_down)

    got = along_z(pack_heads(queries, own, left, right, far))
    mixed = attend(got, kv_count, beam_user, beams)

    part_l, part_r = experts([block_l, block_r], w_up, w_down)
    from_r, from_l = to_left(part_l), to_right(part_r)
    (part_f,) = experts([block_f], w_up, w_down)
    from_f = to_far(part_f)
    ret = along_z(finish(part, from_l, from_r, from_f, mixed), LAST)
    context, routed = combine(ret, routes, route_gate, beams, width)
    return (context, routed)


def solution(mesh):
    return jax.shard_map(
        on_device,
        mesh=mesh,
        in_specs=(
            P(("user", "dev"), None),
            P("user", "dev", None),
            P("user", "dev", None),
            P("user", None),
            P("user"),
            P(("user", "dev"), None),
            P(("user", "dev"), None),
            P(),
            P(None, "dev"),
            P("dev", None),
        ),
        out_specs=(P(("user", "dev"), None), P(("user", "dev"), None)),
        check_vma=False,
    )
```

```python
import functools

import jax
import jax.numpy as jnp
from jax import lax
from jax.experimental import pallas as pl
from jax.experimental.pallas import tpu as pltpu
from jax.sharding import PartitionSpec as P

HEAD = 128
EXPF = 2
CAP = 16
NX = 4
NZ = 8
HALF = NZ // EXPF
BF = jnp.bfloat16
F32 = jnp.float32

FIRST = [0, 4, 1, 5, 2, 6, 3, 7]
LAST = list(range(NZ))[::-1]
RIGHT = [(z * NX + x, z * NX + (x + 1) % NX) for z in range(NZ) for x in range(NX)]
FAR = [(z * NX + x, z * NX + (x + 2) % NX) for z in range(NZ) for x in range(NX)]
LEFT = [(z * NX + x, z * NX + (x - 1) % NX) for z in range(NZ) for x in range(NX)]


def to_right(a):
    return lax.ppermute(a, "dev", RIGHT)


def to_left(a):
    return lax.ppermute(a, "dev", LEFT)


def to_far(a):
    return lax.ppermute(a, "dev", FAR)


def along_z(a, order=tuple(range(NZ))):
    rings = [[z * NX + x for z in order] for x in range(NX)]
    return lax.all_to_all(
        a, "dev", split_axis=0, concat_axis=0, axis_index_groups=rings, tiled=True
    )


def in_hbm(*arrays):
    return [pltpu.with_memory_space_constraint(a, pltpu.HBM) for a in arrays]


def turn(row):
    n = row.shape[1]
    at = lax.broadcasted_iota(jnp.int32, (n, n), 0)
    to = lax.broadcasted_iota(jnp.int32, (n, n), 1)
    return jnp.sum(jnp.where(at == to, row, 0.0), axis=1, keepdims=True)


def pack_rows_kernel(queries_ref, routes_ref, gain_ref, out_ref):
    rows = queries_ref[...].astype(F32)
    mean_sq = jnp.mean(rows * rows, axis=-1, keepdims=True)
    normed = (rows * lax.rsqrt(mean_sq + 1e-06) * gain_ref[...]).astype(BF)
    routes = routes_ref[...]
    beams = rows.shape[0]
    at = lax.broadcasted_iota(jnp.int32, (beams, beams), 0)
    to = lax.broadcasted_iota(jnp.int32, (beams, beams), 1)
    place = lax.broadcasted_iota(jnp.int32, (CAP, beams), 0).astype(F32)
    for expert in range(EXPF):
        mine = jnp.sum((routes == expert).astype(F32), axis=0, keepdims=True)
        slot = jnp.sum(jnp.where(at < to, turn(mine), 0.0), axis=0, keepdims=True)
        picker = jnp.where((place == slot) & (mine > 0.5), 1.0, 0.0).astype(BF)
        packed = jnp.dot(picker, normed, preferred_element_type=F32).astype(BF)
        for z in range(expert * HALF, (expert + 1) * HALF):
            out_ref[FIRST.index(z)] = packed


def pack_rows(queries, routes, gain):
    width = queries.shape[1]
    return pl.pallas_call(
        pack_rows_kernel,
        out_shape=jax.ShapeDtypeStruct((NZ, CAP, width), BF),
        cost_estimate=pl.CostEstimate(
            flops=4_000_000, bytes_accessed=700_000, transcendentals=32
        ),
        compiler_params=pltpu.CompilerParams(vmem_limit_bytes=4 * 2**20),
        name="pack_rows",
    )(*in_hbm(queries, routes, gain.reshape(1, width)))


def finish_kernel(own_ref, left_ref, right_ref, far_ref, out_ref):
    for z in range(NZ):
        rows = slice(FIRST.index(z) * CAP, (FIRST.index(z) + 1) * CAP)
        total = own_ref[rows].astype(F32) + left_ref[rows].astype(F32)
        total = total + right_ref[rows].astype(F32) + far_ref[rows].astype(F32)
        out_ref[LAST.index(z)] = total.astype(BF)


def finish(own, left, right, far):
    return pl.pallas_call(
        finish_kernel,
        out_shape=jax.ShapeDtypeStruct((NZ, CAP, own.shape[1]), BF),
        cost_estimate=pl.CostEstimate(
            flops=1_000_000, bytes_accessed=2_600_000, transcendentals=0
        ),
        compiler_params=pltpu.CompilerParams(vmem_limit_bytes=8 * 2**20),
        name="finish",
    )(own, left, right, far)


def combine_kernel(
    ret_ref, mixed_ref, other_ref, routes_ref, gate_ref, context_ref, routed_ref
):
    routes = routes_ref[...]
    gate = gate_ref[...]
    beams = routes.shape[1]
    at = lax.broadcasted_iota(jnp.int32, (beams, beams), 0)
    to = lax.broadcasted_iota(jnp.int32, (beams, beams), 1)
    place = lax.broadcasted_iota(jnp.int32, (beams, CAP), 1).astype(F32)
    spread = []
    summed = []
    for expert in range(EXPF):
        mine = jnp.sum((routes == expert).astype(F32), axis=0, keepdims=True)
        slot = jnp.sum(jnp.where(to < at, mine, 0.0), axis=1, keepdims=True)
        weight = jnp.sum(jnp.where(routes == expert, gate, 0.0), axis=0, keepdims=True)
        spread.append(jnp.where((place == slot) & (turn(mine) > 0.5), turn(weight), 0.0))
        total = None
        for z in range(expert * HALF, (expert + 1) * HALF):
            term = ret_ref[LAST.index(z)].astype(F32)
            total = term if total is None else total + term
        summed.append(total)
    routed_ref[...] = jnp.dot(
        jnp.concatenate(spread, axis=1),
        jnp.concatenate(summed, axis=0),
        precision=lax.Precision.HIGHEST,
        preferred_element_type=F32,
    ).astype(BF)
    odd = parity() == 1
    for z in range(NZ):
        mine, other = mixed_ref[z, :beams, :], other_ref[z, beams:, :]
        first = 2 * z * HEAD
        context_ref[:, first : first + HEAD] = jnp.where(odd, other, mine)
        context_ref[:, first + HEAD : first + 2 * HEAD] = jnp.where(odd, mine, other)


def combine(ret, mixed, other, routes, gate, beams, width):
    shape = jax.ShapeDtypeStruct((beams, width), BF)
    return pl.pallas_call(
        combine_kernel,
        out_shape=[shape, shape],
        cost_estimate=pl.CostEstimate(
            flops=25_000_000, bytes_accessed=1_000_000, transcendentals=0
        ),
        compiler_params=pltpu.CompilerParams(vmem_limit_bytes=6 * 2**20),
        name="combine",
    )(ret, mixed, other, routes, gate)


def parity():
    return lax.axis_index("dev") % 2


def split_heads_kernel(
    queries_ref, keys_ref, values_ref, right_ref, left_ref, far_ref, mine_ref
):
    odd = parity() == 1
    rows = queries_ref.shape[0]
    for at, ref in enumerate((keys_ref, values_ref, queries_ref)):
        place = slice(at * rows, (at + 1) * rows)
        for z in range(NZ):
            first = ref[:, 2 * z * HEAD : (2 * z + 1) * HEAD]
            second = ref[:, (2 * z + 1) * HEAD : (2 * z + 2) * HEAD]
            same = jnp.where(odd, second, first)
            other = jnp.where(odd, first, second)
            cols = slice(z * HEAD, (z + 1) * HEAD)
            mine_ref[place, cols] = same
            right_ref[place, cols] = other
            if at < 2:
                far_ref[place, cols] = same
                left_ref[place, cols] = other


def split_heads(queries, keys, values):
    rows, width = queries.shape
    three = jax.ShapeDtypeStruct((3 * rows, width // 2), BF)
    two = jax.ShapeDtypeStruct((2 * rows, width // 2), BF)
    return pl.pallas_call(
        split_heads_kernel,
        out_shape=[three, two, two, three],
        cost_estimate=pl.CostEstimate(
            flops=200_000, bytes_accessed=1_700_000, transcendentals=0
        ),
        compiler_params=pltpu.CompilerParams(vmem_limit_bytes=6 * 2**20),
        name="split_heads",
    )(*in_hbm(queries, keys, values))


def pack_heads_kernel(mine_ref, left_ref, right_ref, far_ref, out_ref):
    rows = mine_ref.shape[0] // 3
    for z in range(NZ):
        cols = slice(z * HEAD, (z + 1) * HEAD)
        at = 0
        for which in (0, 1):
            for ref in (mine_ref, left_ref, right_ref, far_ref):
                out_ref[z, at : at + rows, :] = ref[which * rows : (which + 1) * rows, cols]
                at += rows
        for ref in (mine_ref, left_ref):
            out_ref[z, at : at + rows, :] = ref[2 * rows :, cols]
            at += rows


def pack_heads(mine, left, right, far):
    rows = mine.shape[0] // 3
    return pl.pallas_call(
        pack_heads_kernel,
        out_shape=jax.ShapeDtypeStruct((NZ, 2 * (NX + 1) * rows, HEAD), BF),
        cost_estimate=pl.CostEstimate(
            flops=20_000_000_000, bytes_accessed=1_300_000, transcendentals=0
        ),
        compiler_params=pltpu.CompilerParams(vmem_limit_bytes=6 * 2**20),
        name="pack_heads",
    )(mine, left, right, far)


def valid_positions(counts, shard):
    users, shards = counts.shape
    offsets = shard // users
    total = shards * shard
    at = lax.broadcasted_iota(jnp.int32, (shards, total), 1)
    shard_of = at // shard
    step = shard_of % NX
    step = jnp.where(step == 1, NX - 1, jnp.where(step == 2, 1, jnp.where(step == 3, 2, 0)))
    x = (lax.axis_index("dev") + step) % NX
    source = shard_of // NX * NX + x
    spread = (source == lax.broadcasted_iota(jnp.int32, (shards, total), 0)).astype(F32)
    found = jnp.dot(counts.astype(F32), spread, preferred_element_type=F32)
    at = at[:users]
    user = at // offsets % users
    mine = user == lax.broadcasted_iota(jnp.int32, (users, total), 0)
    limit = jnp.sum(jnp.where(mine, found, 0.0), axis=0, keepdims=True)
    return user[:1], (at[:1] % offsets).astype(F32) < limit - 0.5


def attend_kernel(owner_ref, got_ref, counts_ref, out_ref):
    beams = out_ref.shape[1] // 2
    memory = (got_ref.shape[1] - 2 * beams) // 2
    count = NZ * memory
    user, valid = valid_positions(counts_ref[...], memory // NX)
    x = lax.axis_index("dev") % NX
    keys = got_ref[:, 0:memory, :].reshape(count, HEAD)
    values = got_ref[:, memory : 2 * memory, :].reshape(count, HEAD)
    for at, column in enumerate((x, (x + NX - 1) % NX)):
        first = 2 * memory + at * beams
        rows = got_ref[:, first : first + beams, :].reshape(NZ * beams, HEAD)
        scores = lax.dot_general(
            rows, keys, (((1,), (1,)), ((), ())), preferred_element_type=F32
        )
        masked = []
        for src in range(NZ):
            mine = user == owner_ref[src * NX + column]
            bias = jnp.where(mine & valid, 0.0, -1e30)
            masked.append(scores[src * beams : (src + 1) * beams] * HEAD ** (-0.5) + bias)
        scores = jnp.concatenate(masked, axis=0)
        top = jnp.max(scores, axis=-1, keepdims=True)
        expo = jnp.exp(scores - top)
        total = jnp.sum(expo, axis=-1, keepdims=True)
        weights = (expo * (1.0 / total)).astype(BF)
        mixed = jnp.dot(weights, values, preferred_element_type=F32).astype(BF)
        out_ref[:, at * beams : (at + 1) * beams, :] = mixed.reshape(NZ, beams, HEAD)


def attend(got, counts, owner, beams):
    return pl.pallas_call(
        attend_kernel,
        in_specs=[
            pl.BlockSpec(memory_space=pltpu.SMEM),
            pl.BlockSpec(memory_space=pltpu.VMEM),
            pl.BlockSpec(memory_space=pltpu.VMEM),
        ],
        out_shape=jax.ShapeDtypeStruct((NZ, 2 * beams, HEAD), BF),
        cost_estimate=pl.CostEstimate(
            flops=300_000_000, bytes_accessed=1_000_000, transcendentals=600_000
        ),
        compiler_params=pltpu.CompilerParams(vmem_limit_bytes=12 * 2**20),
        name="attend",
    )(owner, got, *in_hbm(counts))


def experts_kernel(*refs):
    *ins, up_ref, down_ref = refs[: len(refs) // 2]
    *outs, up, down, sems = refs[len(refs) // 2 :]
    parts = 2
    copies = []
    for which, (source, target) in enumerate(((up_ref, up), (down_ref, down))):
        size = target.shape[0] // parts
        for part in range(parts):
            own = slice(part * size, (part + 1) * size)
            copies.append(
                pltpu.make_async_copy(source.at[own], target.at[own], sems.at[which, part])
            )
    ahead = 4
    for copy in copies[:ahead]:
        copy.start()
    value = jnp.concatenate([ref[...] for ref in ins], axis=0)
    for which, weight in enumerate((up, down)):
        size = weight.shape[0] // parts
        total = None
        for part in range(parts):
            own = slice(part * size, (part + 1) * size)
            index = which * parts + part
            copies[index].wait()
            if index + ahead < len(copies):
                copies[index + ahead].start()
            term = jnp.dot(value[:, own], weight[own, :], preferred_element_type=F32)
            total = term if total is None else total + term
        if which == 0:
            value = (total / (1.0 + jnp.exp(-total))).astype(BF)
    size = ins[0].shape[0]
    for index, out_ref in enumerate(outs):
        out_ref[...] = total[index * size : (index + 1) * size].astype(BF)


def experts(blocks, up, down):
    count = len(blocks)
    size = count * blocks[0].shape[0]
    width, hidden = up.shape
    return pl.pallas_call(
        experts_kernel,
        in_specs=[pl.BlockSpec(memory_space=pltpu.VMEM)] * count
        + [pl.BlockSpec(memory_space=pl.ANY)] * 2,
        out_shape=[jax.ShapeDtypeStruct(block.shape, BF) for block in blocks],
        scratch_shapes=[
            pltpu.VMEM(up.shape, up.dtype),
            pltpu.VMEM(down.shape, down.dtype),
            pltpu.SemaphoreType.DMA((2, 2)),
        ],
        cost_estimate=pl.CostEstimate(
            flops=400 * size * width * hidden,
            bytes_accessed=4 * width * hidden + 4 * size * width,
            transcendentals=size * hidden,
        ),
        compiler_params=pltpu.CompilerParams(vmem_limit_bytes=14 * 2**20),
        name="experts",
    )(*blocks, *in_hbm(up, down))


def on_device(
    queries, keys, values, kv_count, beam_user, routes, route_gate, norm_gain, w_up, w_down
):
    beams, width = queries.shape
    users, shard_len, _ = keys.shape
    shard = users * shard_len

    routes, route_gate = routes.T, route_gate.T

    size = NZ * CAP
    packed = pack_rows(queries, routes, norm_gain)
    for_right, for_left, for_far, mine = split_heads(
        queries, keys.reshape(shard, width), values.reshape(shard, width)
    )
    left, right, far = to_right(for_right), to_left(for_left), to_far(for_far)
    block = along_z(packed, FIRST).reshape(size, width)
    block, far = lax.optimization_barrier((block, far))
    block_f, block_l, block_r = to_far(block), to_right(block), to_left(block)
    (part,) = experts([block], w_up, w_down)

    got = along_z(pack_heads(mine, left, right, far))
    mixed = along_z(attend(got, kv_count, beam_user, beams))
    other = to_left(mixed)

    (part_f,) = experts([block_f], w_up, w_down)
    from_f = to_far(part_f)
    block_l, block_r, part, _ = lax.optimization_barrier((block_l, block_r, part, part_f))
    part_l, part_r = experts([block_l, block_r], w_up, w_down)
    from_r, from_l = to_left(part_l), to_right(part_r)
    ret = along_z(finish(part, from_l, from_r, from_f), LAST)
    context, routed = combine(ret, mixed, other, routes, route_gate, beams, width)
    return (context, routed)


def solution(mesh):
    return jax.shard_map(
        on_device,
        mesh=mesh,
        in_specs=(
            P(("user", "dev"), None),
            P("user", "dev", None),
            P("user", "dev", None),
            P("user", None),
            P("user"),
            P(("user", "dev"), None),
            P(("user", "dev"), None),
            P(),
            P(None, "dev"),
            P("dev", None),
        ),
        out_specs=(P(("user", "dev"), None), P(("user", "dev"), None)),
        check_vma=False,
    )
```

```python
import functools

import jax
import jax.numpy as jnp
from jax import lax
from jax.experimental import pallas as pl
from jax.experimental.pallas import tpu as pltpu
from jax.sharding import PartitionSpec as P

HEAD = 128
EXPF = 2
CAP = 16
NX = 4
NZ = 8
HALF = NZ // EXPF
BF = jnp.bfloat16
F32 = jnp.float32

FIRST = [0, 4, 1, 5, 2, 6, 3, 7]
LAST = list(range(NZ))[::-1]
RIGHT = [(z * NX + x, z * NX + (x + 1) % NX) for z in range(NZ) for x in range(NX)]
FAR = [(z * NX + x, z * NX + (x + 2) % NX) for z in range(NZ) for x in range(NX)]
LEFT = [(z * NX + x, z * NX + (x - 1) % NX) for z in range(NZ) for x in range(NX)]


def to_right(a):
    return lax.ppermute(a, "dev", RIGHT)


def to_left(a):
    return lax.ppermute(a, "dev", LEFT)


def to_far(a):
    return lax.ppermute(a, "dev", FAR)


def along_z(a, order=tuple(range(NZ))):
    rings = [[z * NX + x for z in order] for x in range(NX)]
    return lax.all_to_all(
        a, "dev", split_axis=0, concat_axis=0, axis_index_groups=rings, tiled=True
    )


def in_hbm(*arrays):
    return [pltpu.with_memory_space_constraint(a, pltpu.HBM) for a in arrays]


def turn(row):
    n = row.shape[1]
    at = lax.broadcasted_iota(jnp.int32, (n, n), 0)
    to = lax.broadcasted_iota(jnp.int32, (n, n), 1)
    return jnp.sum(jnp.where(at == to, row, 0.0), axis=1, keepdims=True)


def pack_rows_kernel(queries_ref, routes_ref, gain_ref, out_ref):
    rows = queries_ref[...].astype(F32)
    mean_sq = jnp.mean(rows * rows, axis=-1, keepdims=True)
    normed = (rows * lax.rsqrt(mean_sq + 1e-06) * gain_ref[...]).astype(BF)
    routes = routes_ref[...]
    beams = rows.shape[0]
    at = lax.broadcasted_iota(jnp.int32, (beams, beams), 0)
    to = lax.broadcasted_iota(jnp.int32, (beams, beams), 1)
    place = lax.broadcasted_iota(jnp.int32, (CAP, beams), 0).astype(F32)
    for expert in range(EXPF):
        mine = jnp.sum((routes == expert).astype(F32), axis=0, keepdims=True)
        slot = jnp.sum(jnp.where(at < to, turn(mine), 0.0), axis=0, keepdims=True)
        picker = jnp.where((place == slot) & (mine > 0.5), 1.0, 0.0).astype(BF)
        packed = jnp.dot(picker, normed, preferred_element_type=F32).astype(BF)
        for z in range(expert * HALF, (expert + 1) * HALF):
            out_ref[FIRST.index(z)] = packed


def pack_rows(queries, routes, gain):
    width = queries.shape[1]
    return pl.pallas_call(
        pack_rows_kernel,
        out_shape=jax.ShapeDtypeStruct((NZ, CAP, width), BF),
        cost_estimate=pl.CostEstimate(
            flops=4_000_000, bytes_accessed=700_000, transcendentals=32
        ),
        compiler_params=pltpu.CompilerParams(vmem_limit_bytes=4 * 2**20),
        name="pack_rows",
    )(*in_hbm(queries, routes, gain.reshape(1, width)))


def gather_kernel(own_ref, far_ref, out_ref):
    out_ref[...] = own_ref[...].astype(F32) + far_ref[...].astype(F32)


def own_and_far(own, far):
    return pl.pallas_call(
        gather_kernel,
        out_shape=jax.ShapeDtypeStruct(own.shape, F32),
        cost_estimate=pl.CostEstimate(
            flops=20_000_000_000, bytes_accessed=2_000_000, transcendentals=0
        ),
        compiler_params=pltpu.CompilerParams(vmem_limit_bytes=8 * 2**20),
        name="own_and_far",
    )(own, far)


def finish_kernel(sum_ref, left_ref, right_ref, out_ref):
    for z in range(NZ):
        rows = slice(FIRST.index(z) * CAP, (FIRST.index(z) + 1) * CAP)
        total = sum_ref[rows] + left_ref[rows].astype(F32) + right_ref[rows].astype(F32)
        out_ref[LAST.index(z)] = total.astype(BF)


def finish(partial, left, right):
    return pl.pallas_call(
        finish_kernel,
        out_shape=jax.ShapeDtypeStruct((NZ, CAP, partial.shape[1]), BF),
        cost_estimate=pl.CostEstimate(
            flops=1_000_000, bytes_accessed=2_600_000, transcendentals=0
        ),
        compiler_params=pltpu.CompilerParams(vmem_limit_bytes=8 * 2**20),
        name="finish",
    )(partial, left, right)


def combine_kernel(
    ret_ref, mixed_ref, other_ref, routes_ref, gate_ref, context_ref, routed_ref
):
    routes = routes_ref[...]
    gate = gate_ref[...]
    beams = routes.shape[1]
    at = lax.broadcasted_iota(jnp.int32, (beams, beams), 0)
    to = lax.broadcasted_iota(jnp.int32, (beams, beams), 1)
    place = lax.broadcasted_iota(jnp.int32, (beams, CAP), 1).astype(F32)
    spread = []
    summed = []
    for expert in range(EXPF):
        mine = jnp.sum((routes == expert).astype(F32), axis=0, keepdims=True)
        slot = jnp.sum(jnp.where(to < at, mine, 0.0), axis=1, keepdims=True)
        weight = jnp.sum(jnp.where(routes == expert, gate, 0.0), axis=0, keepdims=True)
        spread.append(jnp.where((place == slot) & (turn(mine) > 0.5), turn(weight), 0.0))
        total = None
        for z in range(expert * HALF, (expert + 1) * HALF):
            term = ret_ref[LAST.index(z)].astype(F32)
            total = term if total is None else total + term
        summed.append(total)
    routed_ref[...] = jnp.dot(
        jnp.concatenate(spread, axis=1),
        jnp.concatenate(summed, axis=0),
        precision=lax.Precision.HIGHEST,
        preferred_element_type=F32,
    ).astype(BF)
    odd = parity() == 1
    for z in range(NZ):
        mine, other = mixed_ref[z, :beams, :], other_ref[z, beams:, :]
        first = 2 * z * HEAD
        context_ref[:, first : first + HEAD] = jnp.where(odd, other, mine)
        context_ref[:, first + HEAD : first + 2 * HEAD] = jnp.where(odd, mine, other)


def combine(ret, mixed, other, routes, gate, beams, width):
    shape = jax.ShapeDtypeStruct((beams, width), BF)
    return pl.pallas_call(
        combine_kernel,
        out_shape=[shape, shape],
        cost_estimate=pl.CostEstimate(
            flops=25_000_000, bytes_accessed=1_000_000, transcendentals=0
        ),
        compiler_params=pltpu.CompilerParams(vmem_limit_bytes=6 * 2**20),
        name="combine",
    )(ret, mixed, other, routes, gate)


def parity():
    return lax.axis_index("dev") % 2


def split_heads_kernel(
    queries_ref, keys_ref, values_ref, right_ref, left_ref, far_ref, mine_ref
):
    odd = parity() == 1
    rows = queries_ref.shape[0]
    for at, ref in enumerate((keys_ref, values_ref, queries_ref)):
        place = slice(at * rows, (at + 1) * rows)
        for z in range(NZ):
            first = ref[:, 2 * z * HEAD : (2 * z + 1) * HEAD]
            second = ref[:, (2 * z + 1) * HEAD : (2 * z + 2) * HEAD]
            same = jnp.where(odd, second, first)
            other = jnp.where(odd, first, second)
            cols = slice(z * HEAD, (z + 1) * HEAD)
            mine_ref[place, cols] = same
            right_ref[place, cols] = other
            if at < 2:
                far_ref[place, cols] = same
                left_ref[place, cols] = other


def split_heads(queries, keys, values):
    rows, width = queries.shape
    three = jax.ShapeDtypeStruct((3 * rows, width // 2), BF)
    two = jax.ShapeDtypeStruct((2 * rows, width // 2), BF)
    return pl.pallas_call(
        split_heads_kernel,
        out_shape=[three, two, two, three],
        cost_estimate=pl.CostEstimate(
            flops=200_000, bytes_accessed=1_700_000, transcendentals=0
        ),
        compiler_params=pltpu.CompilerParams(vmem_limit_bytes=6 * 2**20),
        name="split_heads",
    )(*in_hbm(queries, keys, values))


def pack_heads_kernel(mine_ref, left_ref, right_ref, far_ref, out_ref):
    rows = mine_ref.shape[0] // 3
    for z in range(NZ):
        cols = slice(z * HEAD, (z + 1) * HEAD)
        at = 0
        for which in (0, 1):
            for ref in (mine_ref, left_ref, right_ref, far_ref):
                out_ref[z, at : at + rows, :] = ref[which * rows : (which + 1) * rows, cols]
                at += rows
        for ref in (mine_ref, left_ref):
            out_ref[z, at : at + rows, :] = ref[2 * rows :, cols]
            at += rows


def pack_heads(mine, left, right, far):
    rows = mine.shape[0] // 3
    return pl.pallas_call(
        pack_heads_kernel,
        out_shape=jax.ShapeDtypeStruct((NZ, 2 * (NX + 1) * rows, HEAD), BF),
        cost_estimate=pl.CostEstimate(
            flops=20_000_000_000, bytes_accessed=1_300_000, transcendentals=0
        ),
        compiler_params=pltpu.CompilerParams(vmem_limit_bytes=6 * 2**20),
        name="pack_heads",
    )(mine, left, right, far)


def valid_positions(counts, shard):
    users, shards = counts.shape
    offsets = shard // users
    total = shards * shard
    at = lax.broadcasted_iota(jnp.int32, (shards, total), 1)
    shard_of = at // shard
    step = shard_of % NX
    step = jnp.where(step == 1, NX - 1, jnp.where(step == 2, 1, jnp.where(step == 3, 2, 0)))
    x = (lax.axis_index("dev") + step) % NX
    source = shard_of // NX * NX + x
    spread = (source == lax.broadcasted_iota(jnp.int32, (shards, total), 0)).astype(F32)
    found = jnp.dot(counts.astype(F32), spread, preferred_element_type=F32)
    at = at[:users]
    user = at // offsets % users
    mine = user == lax.broadcasted_iota(jnp.int32, (users, total), 0)
    limit = jnp.sum(jnp.where(mine, found, 0.0), axis=0, keepdims=True)
    return user[:1], (at[:1] % offsets).astype(F32) < limit - 0.5


def attend_kernel(owner_ref, got_ref, counts_ref, out_ref):
    beams = out_ref.shape[1] // 2
    memory = (got_ref.shape[1] - 2 * beams) // 2
    count = NZ * memory
    user, valid = valid_positions(counts_ref[...], memory // NX)
    x = lax.axis_index("dev") % NX
    keys = got_ref[:, 0:memory, :].reshape(count, HEAD)
    values = got_ref[:, memory : 2 * memory, :].reshape(count, HEAD)
    for at, column in enumerate((x, (x + NX - 1) % NX)):
        first = 2 * memory + at * beams
        rows = got_ref[:, first : first + beams, :].reshape(NZ * beams, HEAD)
        scores = lax.dot_general(
            rows, keys, (((1,), (1,)), ((), ())), preferred_element_type=F32
        )
        masked = []
        for src in range(NZ):
            mine = user == owner_ref[src * NX + column]
            bias = jnp.where(mine & valid, 0.0, -1e30)
            masked.append(scores[src * beams : (src + 1) * beams] * HEAD ** (-0.5) + bias)
        scores = jnp.concatenate(masked, axis=0)
        top = jnp.max(scores, axis=-1, keepdims=True)
        expo = jnp.exp(scores - top)
        total = jnp.sum(expo, axis=-1, keepdims=True)
        weights = (expo * (1.0 / total)).astype(BF)
        mixed = jnp.dot(weights, values, preferred_element_type=F32).astype(BF)
        out_ref[:, at * beams : (at + 1) * beams, :] = mixed.reshape(NZ, beams, HEAD)


def attend(got, counts, owner, beams):
    return pl.pallas_call(
        attend_kernel,
        in_specs=[
            pl.BlockSpec(memory_space=pltpu.SMEM),
            pl.BlockSpec(memory_space=pltpu.VMEM),
            pl.BlockSpec(memory_space=pltpu.VMEM),
        ],
        out_shape=jax.ShapeDtypeStruct((NZ, 2 * beams, HEAD), BF),
        cost_estimate=pl.CostEstimate(
            flops=300_000_000, bytes_accessed=1_000_000, transcendentals=600_000
        ),
        compiler_params=pltpu.CompilerParams(vmem_limit_bytes=12 * 2**20),
        name="attend",
    )(owner, got, *in_hbm(counts))


def preload_kernel(up_ref, down_ref, up_out, down_out, sems):
    copies = [
        pltpu.make_async_copy(source, target, sems.at[at])
        for at, (source, target) in enumerate(((up_ref, up_out), (down_ref, down_out)))
    ]
    for copy in copies:
        copy.start()
    for copy in copies:
        copy.wait()


def preload(up, down):
    return pl.pallas_call(
        preload_kernel,
        in_specs=[pl.BlockSpec(memory_space=pl.ANY)] * 2,
        out_specs=[pl.BlockSpec(memory_space=pltpu.VMEM)] * 2,
        out_shape=[jax.ShapeDtypeStruct(a.shape, a.dtype) for a in (up, down)],
        scratch_shapes=[pltpu.SemaphoreType.DMA((2,))],
        cost_estimate=pl.CostEstimate(flops=0, bytes_accessed=8 * 2**20, transcendentals=0),
        compiler_params=pltpu.CompilerParams(vmem_limit_bytes=6 * 2**20),
        name="preload",
    )(*in_hbm(up, down))


def experts_kernel(*refs):
    *ins, up_ref, down_ref = refs[: len(refs) // 2 + 1]
    outs = refs[len(refs) // 2 + 1 :]
    rows = jnp.concatenate([ref[...] for ref in ins], axis=0)
    hidden = jnp.dot(rows, up_ref[...], preferred_element_type=F32)
    hidden = (hidden / (1.0 + jnp.exp(-hidden))).astype(BF)
    total = jnp.dot(hidden, down_ref[...], preferred_element_type=F32).astype(BF)
    size = ins[0].shape[0]
    for index, out_ref in enumerate(outs):
        out_ref[...] = total[index * size : (index + 1) * size]


def experts(blocks, up, down):
    count = len(blocks)
    size = count * blocks[0].shape[0]
    width, hidden = up.shape
    return pl.pallas_call(
        experts_kernel,
        in_specs=[pl.BlockSpec(memory_space=pltpu.VMEM)] * (count + 2),
        out_shape=[jax.ShapeDtypeStruct(block.shape, BF) for block in blocks],
        cost_estimate=pl.CostEstimate(
            flops=400 * size * width * hidden,
            bytes_accessed=4 * width * hidden + 4 * size * width,
            transcendentals=size * hidden,
        ),
        compiler_params=pltpu.CompilerParams(vmem_limit_bytes=10 * 2**20),
        name="experts",
    )(*blocks, up, down)


def on_device(
    queries, keys, values, kv_count, beam_user, routes, route_gate, norm_gain, w_up, w_down
):
    beams, width = queries.shape
    users, shard_len, _ = keys.shape
    shard = users * shard_len

    routes, route_gate = routes.T, route_gate.T

    size = NZ * CAP
    packed = pack_rows(queries, routes, norm_gain)
    for_right, for_left, for_far, mine = split_heads(
        queries, keys.reshape(shard, width), values.reshape(shard, width)
    )
    left, right, far = to_right(for_right), to_left(for_left), to_far(for_far)
    block = along_z(packed, FIRST).reshape(size, width)
    block, far = lax.optimization_barrier((block, far))
    block_f, block_l, block_r = to_far(block), to_right(block), to_left(block)
    w_up, w_down, _ = lax.optimization_barrier((w_up, w_down, block))
    w_up, w_down = preload(w_up, w_down)
    (part,) = experts([block], w_up, w_down)

    got = along_z(pack_heads(mine, left, right, far))
    mixed = along_z(attend(got, kv_count, beam_user, beams))
    other = to_left(mixed)

    (part_f,) = experts([block_f], w_up, w_down)
    from_f = to_far(part_f)
    block_l, block_r, part, _ = lax.optimization_barrier((block_l, block_r, part, part_f))
    part_l, part_r = experts([block_l, block_r], w_up, w_down)
    from_r, from_l = to_left(part_l), to_right(part_r)
    ret = along_z(finish(own_and_far(part, from_f), from_l, from_r), LAST)
    context, routed = combine(ret, mixed, other, routes, route_gate, beams, width)
    return (context, routed)


def solution(mesh):
    return jax.shard_map(
        on_device,
        mesh=mesh,
        in_specs=(
            P(("user", "dev"), None),
            P("user", "dev", None),
            P("user", "dev", None),
            P("user", None),
            P("user"),
            P(("user", "dev"), None),
            P(("user", "dev"), None),
            P(),
            P(None, "dev"),
            P("dev", None),
        ),
        out_specs=(P(("user", "dev"), None), P(("user", "dev"), None)),
        check_vma=False,
    )
```

```python
import functools

import jax
import jax.numpy as jnp
from jax import lax
from jax.experimental import pallas as pl
from jax.experimental.pallas import tpu as pltpu
from jax.sharding import PartitionSpec as P

HEAD = 128
EXPF = 2
CAP = 16
NX = 4
NZ = 8
HALF = NZ // EXPF
BF = jnp.bfloat16
F32 = jnp.float32

FIRST = [0, 4, 1, 5, 2, 6, 3, 7]
LAST = list(range(NZ))[::-1]
RIGHT = [(z * NX + x, z * NX + (x + 1) % NX) for z in range(NZ) for x in range(NX)]
FAR = [(z * NX + x, z * NX + (x + 2) % NX) for z in range(NZ) for x in range(NX)]
LEFT = [(z * NX + x, z * NX + (x - 1) % NX) for z in range(NZ) for x in range(NX)]


def to_right(a):
    return lax.ppermute(a, "dev", RIGHT)


def to_left(a):
    return lax.ppermute(a, "dev", LEFT)


def to_far(a):
    return lax.ppermute(a, "dev", FAR)


def along_z(a, order=tuple(range(NZ))):
    rings = [[z * NX + x for z in order] for x in range(NX)]
    return lax.all_to_all(
        a, "dev", split_axis=0, concat_axis=0, axis_index_groups=rings, tiled=True
    )


def in_hbm(*arrays):
    return [pltpu.with_memory_space_constraint(a, pltpu.HBM) for a in arrays]


def turn(row):
    n = row.shape[1]
    at = lax.broadcasted_iota(jnp.int32, (n, n), 0)
    to = lax.broadcasted_iota(jnp.int32, (n, n), 1)
    return jnp.sum(jnp.where(at == to, row, 0.0), axis=1, keepdims=True)


def pack_rows_kernel(queries_ref, routes_ref, gain_ref, out_ref):
    rows = queries_ref[...].astype(F32)
    mean_sq = jnp.mean(rows * rows, axis=-1, keepdims=True)
    normed = (rows * lax.rsqrt(mean_sq + 1e-06) * gain_ref[...]).astype(BF)
    routes = routes_ref[...]
    beams = rows.shape[0]
    at = lax.broadcasted_iota(jnp.int32, (beams, beams), 0)
    to = lax.broadcasted_iota(jnp.int32, (beams, beams), 1)
    place = lax.broadcasted_iota(jnp.int32, (CAP, beams), 0).astype(F32)
    for expert in range(EXPF):
        mine = jnp.sum((routes == expert).astype(F32), axis=0, keepdims=True)
        slot = jnp.sum(jnp.where(at < to, turn(mine), 0.0), axis=0, keepdims=True)
        picker = jnp.where((place == slot) & (mine > 0.5), 1.0, 0.0).astype(BF)
        packed = jnp.dot(picker, normed, preferred_element_type=F32).astype(BF)
        for z in range(expert * HALF, (expert + 1) * HALF):
            out_ref[FIRST.index(z)] = packed


def pack_rows(queries, routes, gain):
    width = queries.shape[1]
    return pl.pallas_call(
        pack_rows_kernel,
        out_shape=jax.ShapeDtypeStruct((NZ, CAP, width), BF),
        cost_estimate=pl.CostEstimate(
            flops=4_000_000, bytes_accessed=700_000, transcendentals=32
        ),
        compiler_params=pltpu.CompilerParams(vmem_limit_bytes=4 * 2**20),
        name="pack_rows",
    )(*in_hbm(queries, routes, gain.reshape(1, width)))


def gather_kernel(own_ref, far_ref, out_ref):
    out_ref[...] = own_ref[...].astype(F32) + far_ref[...].astype(F32)


def own_and_far(own, far):
    return pl.pallas_call(
        gather_kernel,
        out_shape=jax.ShapeDtypeStruct(own.shape, F32),
        cost_estimate=pl.CostEstimate(
            flops=20_000_000_000, bytes_accessed=2_000_000, transcendentals=0
        ),
        compiler_params=pltpu.CompilerParams(vmem_limit_bytes=8 * 2**20),
        name="own_and_far",
    )(own, far)


def finish_kernel(sum_ref, left_ref, right_ref, out_ref):
    for z in range(NZ):
        rows = slice(FIRST.index(z) * CAP, (FIRST.index(z) + 1) * CAP)
        total = sum_ref[rows] + left_ref[rows].astype(F32) + right_ref[rows].astype(F32)
        out_ref[LAST.index(z)] = total.astype(BF)


def finish(partial, left, right):
    return pl.pallas_call(
        finish_kernel,
        out_shape=jax.ShapeDtypeStruct((NZ, CAP, partial.shape[1]), BF),
        cost_estimate=pl.CostEstimate(
            flops=1_000_000, bytes_accessed=2_600_000, transcendentals=0
        ),
        compiler_params=pltpu.CompilerParams(vmem_limit_bytes=8 * 2**20),
        name="finish",
    )(partial, left, right)


def prepare_kernel(mixed_ref, other_ref, routes_ref, gate_ref, context_ref, spread_ref):
    routes = routes_ref[...]
    gate = gate_ref[...]
    beams = routes.shape[1]
    at = lax.broadcasted_iota(jnp.int32, (beams, beams), 0)
    to = lax.broadcasted_iota(jnp.int32, (beams, beams), 1)
    place = lax.broadcasted_iota(jnp.int32, (beams, CAP), 1).astype(F32)
    spread = []
    for expert in range(EXPF):
        mine = jnp.sum((routes == expert).astype(F32), axis=0, keepdims=True)
        slot = jnp.sum(jnp.where(to < at, mine, 0.0), axis=1, keepdims=True)
        weight = jnp.sum(jnp.where(routes == expert, gate, 0.0), axis=0, keepdims=True)
        spread.append(jnp.where((place == slot) & (turn(mine) > 0.5), turn(weight), 0.0))
    spread_ref[...] = jnp.concatenate(spread, axis=1)
    odd = parity() == 1
    for z in range(NZ):
        mine, other = mixed_ref[z, :beams, :], other_ref[z, beams:, :]
        first = 2 * z * HEAD
        context_ref[:, first : first + HEAD] = jnp.where(odd, other, mine)
        context_ref[:, first + HEAD : first + 2 * HEAD] = jnp.where(odd, mine, other)


def prepare(mixed, other, routes, gate, beams, width):
    return pl.pallas_call(
        prepare_kernel,
        out_shape=[
            jax.ShapeDtypeStruct((beams, width), BF),
            jax.ShapeDtypeStruct((beams, EXPF * CAP), F32),
        ],
        cost_estimate=pl.CostEstimate(
            flops=100_000, bytes_accessed=400_000, transcendentals=0
        ),
        compiler_params=pltpu.CompilerParams(vmem_limit_bytes=4 * 2**20),
        name="prepare",
    )(mixed, other, routes, gate)


def combine_kernel(ret_ref, spread_ref, routed_ref):
    summed = []
    for expert in range(EXPF):
        total = None
        for z in range(expert * HALF, (expert + 1) * HALF):
            term = ret_ref[LAST.index(z)].astype(F32)
            total = term if total is None else total + term
        summed.append(total)
    routed_ref[...] = jnp.dot(
        spread_ref[...],
        jnp.concatenate(summed, axis=0),
        precision=lax.Precision.HIGHEST,
        preferred_element_type=F32,
    ).astype(BF)


def combine(ret, spread, beams, width):
    return pl.pallas_call(
        combine_kernel,
        out_shape=jax.ShapeDtypeStruct((beams, width), BF),
        cost_estimate=pl.CostEstimate(
            flops=25_000_000, bytes_accessed=1_000_000, transcendentals=0
        ),
        compiler_params=pltpu.CompilerParams(vmem_limit_bytes=6 * 2**20),
        name="combine",
    )(ret, spread)


def parity():
    return lax.axis_index("dev") % 2


def split_heads_kernel(
    queries_ref, keys_ref, values_ref, right_ref, left_ref, far_ref, mine_ref
):
    odd = parity() == 1
    rows = queries_ref.shape[0]
    for at, ref in enumerate((keys_ref, values_ref, queries_ref)):
        place = slice(at * rows, (at + 1) * rows)
        for z in range(NZ):
            first = ref[:, 2 * z * HEAD : (2 * z + 1) * HEAD]
            second = ref[:, (2 * z + 1) * HEAD : (2 * z + 2) * HEAD]
            same = jnp.where(odd, second, first)
            other = jnp.where(odd, first, second)
            cols = slice(z * HEAD, (z + 1) * HEAD)
            mine_ref[place, cols] = same
            right_ref[place, cols] = other
            if at < 2:
                far_ref[place, cols] = same
                left_ref[place, cols] = other


def split_heads(queries, keys, values):
    rows, width = queries.shape
    three = jax.ShapeDtypeStruct((3 * rows, width // 2), BF)
    two = jax.ShapeDtypeStruct((2 * rows, width // 2), BF)
    return pl.pallas_call(
        split_heads_kernel,
        out_shape=[three, two, two, three],
        cost_estimate=pl.CostEstimate(
            flops=200_000, bytes_accessed=1_700_000, transcendentals=0
        ),
        compiler_params=pltpu.CompilerParams(vmem_limit_bytes=6 * 2**20),
        name="split_heads",
    )(*in_hbm(queries, keys, values))


def pack_heads_kernel(mine_ref, left_ref, right_ref, far_ref, out_ref):
    rows = mine_ref.shape[0] // 3
    for z in range(NZ):
        cols = slice(z * HEAD, (z + 1) * HEAD)
        at = 0
        for which in (0, 1):
            for ref in (mine_ref, left_ref, right_ref, far_ref):
                out_ref[z, at : at + rows, :] = ref[which * rows : (which + 1) * rows, cols]
                at += rows
        for ref in (mine_ref, left_ref):
            out_ref[z, at : at + rows, :] = ref[2 * rows :, cols]
            at += rows


def pack_heads(mine, left, right, far):
    rows = mine.shape[0] // 3
    return pl.pallas_call(
        pack_heads_kernel,
        out_shape=jax.ShapeDtypeStruct((NZ, 2 * (NX + 1) * rows, HEAD), BF),
        cost_estimate=pl.CostEstimate(
            flops=20_000_000_000, bytes_accessed=1_300_000, transcendentals=0
        ),
        compiler_params=pltpu.CompilerParams(vmem_limit_bytes=6 * 2**20),
        name="pack_heads",
    )(mine, left, right, far)


def valid_positions(counts, shard):
    users, shards = counts.shape
    offsets = shard // users
    total = shards * shard
    at = lax.broadcasted_iota(jnp.int32, (shards, total), 1)
    shard_of = at // shard
    step = shard_of % NX
    step = jnp.where(step == 1, NX - 1, jnp.where(step == 2, 1, jnp.where(step == 3, 2, 0)))
    x = (lax.axis_index("dev") + step) % NX
    source = shard_of // NX * NX + x
    spread = (source == lax.broadcasted_iota(jnp.int32, (shards, total), 0)).astype(F32)
    found = jnp.dot(counts.astype(F32), spread, preferred_element_type=F32)
    at = at[:users]
    user = at // offsets % users
    mine = user == lax.broadcasted_iota(jnp.int32, (users, total), 0)
    limit = jnp.sum(jnp.where(mine, found, 0.0), axis=0, keepdims=True)
    return user[:1], (at[:1] % offsets).astype(F32) < limit - 0.5


def attend_kernel(owner_ref, got_ref, counts_ref, out_ref):
    beams = out_ref.shape[1] // 2
    memory = (got_ref.shape[1] - 2 * beams) // 2
    count = NZ * memory
    user, valid = valid_positions(counts_ref[...], memory // NX)
    x = lax.axis_index("dev") % NX
    keys = got_ref[:, 0:memory, :].reshape(count, HEAD)
    values = got_ref[:, memory : 2 * memory, :].reshape(count, HEAD)
    for at, column in enumerate((x, (x + NX - 1) % NX)):
        first = 2 * memory + at * beams
        rows = got_ref[:, first : first + beams, :].reshape(NZ * beams, HEAD)
        scores = lax.dot_general(
            rows, keys, (((1,), (1,)), ((), ())), preferred_element_type=F32
        )
        masked = []
        for src in range(NZ):
            mine = user == owner_ref[src * NX + column]
            bias = jnp.where(mine & valid, 0.0, -1e30)
            masked.append(scores[src * beams : (src + 1) * beams] * HEAD ** (-0.5) + bias)
        scores = jnp.concatenate(masked, axis=0)
        top = jnp.max(scores, axis=-1, keepdims=True)
        expo = jnp.exp(scores - top)
        total = jnp.sum(expo, axis=-1, keepdims=True)
        weights = (expo * (1.0 / total)).astype(BF)
        mixed = jnp.dot(weights, values, preferred_element_type=F32).astype(BF)
        out_ref[:, at * beams : (at + 1) * beams, :] = mixed.reshape(NZ, beams, HEAD)


def attend(got, counts, owner, beams):
    return pl.pallas_call(
        attend_kernel,
        in_specs=[
            pl.BlockSpec(memory_space=pltpu.SMEM),
            pl.BlockSpec(memory_space=pltpu.VMEM),
            pl.BlockSpec(memory_space=pltpu.VMEM),
        ],
        out_shape=jax.ShapeDtypeStruct((NZ, 2 * beams, HEAD), BF),
        cost_estimate=pl.CostEstimate(
            flops=300_000_000, bytes_accessed=1_000_000, transcendentals=600_000
        ),
        compiler_params=pltpu.CompilerParams(vmem_limit_bytes=12 * 2**20),
        name="attend",
    )(owner, got, *in_hbm(counts))


def preload_kernel(up_ref, down_ref, up_out, down_out, sems):
    copies = [
        pltpu.make_async_copy(source, target, sems.at[at])
        for at, (source, target) in enumerate(((up_ref, up_out), (down_ref, down_out)))
    ]
    for copy in copies:
        copy.start()
    for copy in copies:
        copy.wait()


def preload(up, down):
    return pl.pallas_call(
        preload_kernel,
        in_specs=[pl.BlockSpec(memory_space=pl.ANY)] * 2,
        out_specs=[pl.BlockSpec(memory_space=pltpu.VMEM)] * 2,
        out_shape=[jax.ShapeDtypeStruct(a.shape, a.dtype) for a in (up, down)],
        scratch_shapes=[pltpu.SemaphoreType.DMA((2,))],
        cost_estimate=pl.CostEstimate(flops=0, bytes_accessed=8 * 2**20, transcendentals=0),
        compiler_params=pltpu.CompilerParams(vmem_limit_bytes=6 * 2**20),
        name="preload",
    )(*in_hbm(up, down))


def experts_kernel(*refs):
    *ins, up_ref, down_ref = refs[: len(refs) // 2 + 1]
    outs = refs[len(refs) // 2 + 1 :]
    rows = jnp.concatenate([ref[...] for ref in ins], axis=0)
    hidden = jnp.dot(rows, up_ref[...], preferred_element_type=F32)
    hidden = (hidden / (1.0 + jnp.exp(-hidden))).astype(BF)
    total = jnp.dot(hidden, down_ref[...], preferred_element_type=F32).astype(BF)
    size = ins[0].shape[0]
    for index, out_ref in enumerate(outs):
        out_ref[...] = total[index * size : (index + 1) * size]


def experts(blocks, up, down):
    count = len(blocks)
    size = count * blocks[0].shape[0]
    width, hidden = up.shape
    return pl.pallas_call(
        experts_kernel,
        in_specs=[pl.BlockSpec(memory_space=pltpu.VMEM)] * (count + 2),
        out_shape=[jax.ShapeDtypeStruct(block.shape, BF) for block in blocks],
        cost_estimate=pl.CostEstimate(
            flops=400 * size * width * hidden,
            bytes_accessed=4 * width * hidden + 4 * size * width,
            transcendentals=size * hidden,
        ),
        compiler_params=pltpu.CompilerParams(vmem_limit_bytes=10 * 2**20),
        name="experts",
    )(*blocks, up, down)


def on_device(
    queries, keys, values, kv_count, beam_user, routes, route_gate, norm_gain, w_up, w_down
):
    beams, width = queries.shape
    users, shard_len, _ = keys.shape
    shard = users * shard_len

    routes, route_gate = routes.T, route_gate.T

    size = NZ * CAP
    packed = pack_rows(queries, routes, norm_gain)
    for_right, for_left, for_far, mine = split_heads(
        queries, keys.reshape(shard, width), values.reshape(shard, width)
    )
    left, right, far = to_right(for_right), to_left(for_left), to_far(for_far)
    block = along_z(packed, FIRST).reshape(size, width)
    block, far = lax.optimization_barrier((block, far))
    block_f, block_l, block_r = to_far(block), to_right(block), to_left(block)
    w_up, w_down, _ = lax.optimization_barrier((w_up, w_down, block))
    w_up, w_down = preload(w_up, w_down)
    (part,) = experts([block], w_up, w_down)

    got = along_z(pack_heads(mine, left, right, far))
    mixed = along_z(attend(got, kv_count, beam_user, beams))
    other = to_left(mixed)

    (part_f,) = experts([block_f], w_up, w_down)
    from_f = to_far(part_f)
    block_l, block_r, part, _ = lax.optimization_barrier((block_l, block_r, part, part_f))
    part_l, part_r = experts([block_l, block_r], w_up, w_down)
    from_r, from_l = to_left(part_l), to_right(part_r)
    ret = along_z(finish(own_and_far(part, from_f), from_l, from_r), LAST)
    context, spread = prepare(mixed, other, routes, route_gate, beams, width)
    routed = combine(ret, spread, beams, width)
    return (context, routed)


def solution(mesh):
    return jax.shard_map(
        on_device,
        mesh=mesh,
        in_specs=(
            P(("user", "dev"), None),
            P("user", "dev", None),
            P("user", "dev", None),
            P("user", None),
            P("user"),
            P(("user", "dev"), None),
            P(("user", "dev"), None),
            P(),
            P(None, "dev"),
            P("dev", None),
        ),
        out_specs=(P(("user", "dev"), None), P(("user", "dev"), None)),
        check_vma=False,
    )
```

```python
import functools

import jax
import jax.numpy as jnp
from jax import lax
from jax.experimental import pallas as pl
from jax.experimental.pallas import tpu as pltpu
from jax.sharding import PartitionSpec as P

HEAD = 128
EXPF = 2
CAP = 16
NX = 4
NZ = 8
HALF = NZ // EXPF
BF = jnp.bfloat16
F32 = jnp.float32

FIRST = [0, 4, 1, 5, 2, 6, 3, 7]
LAST = list(range(NZ))[::-1]
RIGHT = [(z * NX + x, z * NX + (x + 1) % NX) for z in range(NZ) for x in range(NX)]
FAR = [(z * NX + x, z * NX + (x + 2) % NX) for z in range(NZ) for x in range(NX)]
LEFT = [(z * NX + x, z * NX + (x - 1) % NX) for z in range(NZ) for x in range(NX)]


def to_right(a):
    return lax.ppermute(a, "dev", RIGHT)


def to_left(a):
    return lax.ppermute(a, "dev", LEFT)


def to_far(a):
    return lax.ppermute(a, "dev", FAR)


def along_z(a, order=tuple(range(NZ))):
    rings = [[z * NX + x for z in order] for x in range(NX)]
    return lax.all_to_all(
        a, "dev", split_axis=0, concat_axis=0, axis_index_groups=rings, tiled=True
    )


def in_hbm(*arrays):
    return [pltpu.with_memory_space_constraint(a, pltpu.HBM) for a in arrays]


def turn(row):
    n = row.shape[1]
    at = lax.broadcasted_iota(jnp.int32, (n, n), 0)
    to = lax.broadcasted_iota(jnp.int32, (n, n), 1)
    return jnp.sum(jnp.where(at == to, row, 0.0), axis=1, keepdims=True)


def pack_rows_kernel(queries_ref, routes_ref, gain_ref, out_ref):
    rows = queries_ref[...].astype(F32)
    mean_sq = jnp.mean(rows * rows, axis=-1, keepdims=True)
    normed = (rows * lax.rsqrt(mean_sq + 1e-06) * gain_ref[...]).astype(BF)
    routes = routes_ref[...]
    beams = rows.shape[0]
    at = lax.broadcasted_iota(jnp.int32, (beams, beams), 0)
    to = lax.broadcasted_iota(jnp.int32, (beams, beams), 1)
    place = lax.broadcasted_iota(jnp.int32, (CAP, beams), 0).astype(F32)
    for expert in range(EXPF):
        mine = jnp.sum((routes == expert).astype(F32), axis=0, keepdims=True)
        slot = jnp.sum(jnp.where(at < to, turn(mine), 0.0), axis=0, keepdims=True)
        picker = jnp.where((place == slot) & (mine > 0.5), 1.0, 0.0).astype(BF)
        packed = jnp.dot(picker, normed, preferred_element_type=F32).astype(BF)
        for z in range(expert * HALF, (expert + 1) * HALF):
            out_ref[FIRST.index(z)] = packed


def pack_rows(queries, routes, gain):
    width = queries.shape[1]
    return pl.pallas_call(
        pack_rows_kernel,
        out_shape=jax.ShapeDtypeStruct((NZ, CAP, width), BF),
        cost_estimate=pl.CostEstimate(
            flops=4_000_000, bytes_accessed=700_000, transcendentals=32
        ),
        compiler_params=pltpu.CompilerParams(vmem_limit_bytes=4 * 2**20),
        name="pack_rows",
    )(*in_hbm(queries, routes, gain.reshape(1, width)))


def gather_kernel(own_ref, far_ref, out_ref):
    out_ref[...] = own_ref[...].astype(F32) + far_ref[...].astype(F32)


def own_and_far(own, far):
    return pl.pallas_call(
        gather_kernel,
        out_shape=jax.ShapeDtypeStruct(own.shape, F32),
        cost_estimate=pl.CostEstimate(
            flops=20_000_000_000, bytes_accessed=2_000_000, transcendentals=0
        ),
        compiler_params=pltpu.CompilerParams(vmem_limit_bytes=8 * 2**20),
        name="own_and_far",
    )(own, far)


def finish_kernel(sum_ref, left_ref, right_ref, out_ref):
    for z in range(NZ):
        rows = slice(FIRST.index(z) * CAP, (FIRST.index(z) + 1) * CAP)
        total = sum_ref[rows] + left_ref[rows].astype(F32) + right_ref[rows].astype(F32)
        out_ref[LAST.index(z)] = total.astype(BF)


def finish(partial, left, right):
    return pl.pallas_call(
        finish_kernel,
        out_shape=jax.ShapeDtypeStruct((NZ, CAP, partial.shape[1]), BF),
        cost_estimate=pl.CostEstimate(
            flops=1_000_000, bytes_accessed=2_600_000, transcendentals=0
        ),
        compiler_params=pltpu.CompilerParams(vmem_limit_bytes=8 * 2**20),
        name="finish",
    )(partial, left, right)


def combine_kernel(
    ret_ref, mixed_ref, other_ref, routes_ref, gate_ref, context_ref, routed_ref
):
    routes = routes_ref[...]
    gate = gate_ref[...]
    beams = routes.shape[1]
    at = lax.broadcasted_iota(jnp.int32, (beams, beams), 0)
    to = lax.broadcasted_iota(jnp.int32, (beams, beams), 1)
    place = lax.broadcasted_iota(jnp.int32, (beams, CAP), 1).astype(F32)
    spread = []
    summed = []
    for expert in range(EXPF):
        mine = jnp.sum((routes == expert).astype(F32), axis=0, keepdims=True)
        slot = jnp.sum(jnp.where(to < at, mine, 0.0), axis=1, keepdims=True)
        weight = jnp.sum(jnp.where(routes == expert, gate, 0.0), axis=0, keepdims=True)
        spread.append(jnp.where((place == slot) & (turn(mine) > 0.5), turn(weight), 0.0))
        total = None
        for z in range(expert * HALF, (expert + 1) * HALF):
            term = ret_ref[LAST.index(z)].astype(F32)
            total = term if total is None else total + term
        summed.append(total)
    routed_ref[...] = jnp.dot(
        jnp.concatenate(spread, axis=1),
        jnp.concatenate(summed, axis=0),
        precision=lax.Precision.HIGHEST,
        preferred_element_type=F32,
    ).astype(BF)
    odd = parity() == 1
    for z in range(NZ):
        mine, other = mixed_ref[z, :beams, :], other_ref[z, beams:, :]
        first = 2 * z * HEAD
        context_ref[:, first : first + HEAD] = jnp.where(odd, other, mine)
        context_ref[:, first + HEAD : first + 2 * HEAD] = jnp.where(odd, mine, other)


def combine(ret, mixed, other, routes, gate, beams, width):
    shape = jax.ShapeDtypeStruct((beams, width), BF)
    return pl.pallas_call(
        combine_kernel,
        out_shape=[shape, shape],
        cost_estimate=pl.CostEstimate(
            flops=25_000_000, bytes_accessed=1_000_000, transcendentals=0
        ),
        compiler_params=pltpu.CompilerParams(vmem_limit_bytes=6 * 2**20),
        name="combine",
    )(ret, mixed, other, routes, gate)


def parity():
    return lax.axis_index("dev") % 2


def split_heads_kernel(
    queries_ref, keys_ref, values_ref, right_ref, left_ref, far_ref, mine_ref
):
    odd = parity() == 1
    rows = queries_ref.shape[0]
    for at, ref in enumerate((keys_ref, values_ref, queries_ref)):
        place = slice(at * rows, (at + 1) * rows)
        for z in range(NZ):
            first = ref[:, 2 * z * HEAD : (2 * z + 1) * HEAD]
            second = ref[:, (2 * z + 1) * HEAD : (2 * z + 2) * HEAD]
            same = jnp.where(odd, second, first)
            other = jnp.where(odd, first, second)
            cols = slice(z * HEAD, (z + 1) * HEAD)
            mine_ref[place, cols] = same
            right_ref[place, cols] = other
            if at < 2:
                far_ref[place, cols] = same
                left_ref[place, cols] = other


def split_heads(queries, keys, values):
    rows, width = queries.shape
    three = jax.ShapeDtypeStruct((3 * rows, width // 2), BF)
    two = jax.ShapeDtypeStruct((2 * rows, width // 2), BF)
    return pl.pallas_call(
        split_heads_kernel,
        out_shape=[three, two, two, three],
        cost_estimate=pl.CostEstimate(
            flops=200_000, bytes_accessed=1_700_000, transcendentals=0
        ),
        compiler_params=pltpu.CompilerParams(vmem_limit_bytes=6 * 2**20),
        name="split_heads",
    )(*in_hbm(queries, keys, values))


def pack_heads_kernel(mine_ref, left_ref, right_ref, far_ref, out_ref):
    rows = mine_ref.shape[0] // 3
    for z in range(NZ):
        cols = slice(z * HEAD, (z + 1) * HEAD)
        at = 0
        for which in (0, 1):
            for ref in (mine_ref, left_ref, right_ref, far_ref):
                out_ref[z, at : at + rows, :] = ref[which * rows : (which + 1) * rows, cols]
                at += rows
        for ref in (mine_ref, left_ref):
            out_ref[z, at : at + rows, :] = ref[2 * rows :, cols]
            at += rows


def pack_heads(mine, left, right, far):
    rows = mine.shape[0] // 3
    return pl.pallas_call(
        pack_heads_kernel,
        out_shape=jax.ShapeDtypeStruct((NZ, 2 * (NX + 1) * rows, HEAD), BF),
        cost_estimate=pl.CostEstimate(
            flops=20_000_000_000, bytes_accessed=1_300_000, transcendentals=0
        ),
        compiler_params=pltpu.CompilerParams(vmem_limit_bytes=6 * 2**20),
        name="pack_heads",
    )(mine, left, right, far)


def valid_positions(counts, shard):
    users, shards = counts.shape
    offsets = shard // users
    total = shards * shard
    at = lax.broadcasted_iota(jnp.int32, (shards, total), 1)
    shard_of = at // shard
    step = shard_of % NX
    step = jnp.where(step == 1, NX - 1, jnp.where(step == 2, 1, jnp.where(step == 3, 2, 0)))
    x = (lax.axis_index("dev") + step) % NX
    source = shard_of // NX * NX + x
    spread = (source == lax.broadcasted_iota(jnp.int32, (shards, total), 0)).astype(F32)
    found = jnp.dot(counts.astype(F32), spread, preferred_element_type=F32)
    at = at[:users]
    user = at // offsets % users
    mine = user == lax.broadcasted_iota(jnp.int32, (users, total), 0)
    limit = jnp.sum(jnp.where(mine, found, 0.0), axis=0, keepdims=True)
    return user[:1], (at[:1] % offsets).astype(F32) < limit - 0.5


def attend_kernel(owner_ref, got_ref, counts_ref, out_ref):
    beams = out_ref.shape[1] // 2
    memory = (got_ref.shape[1] - 2 * beams) // 2
    count = NZ * memory
    user, valid = valid_positions(counts_ref[...], memory // NX)
    x = lax.axis_index("dev") % NX
    keys = got_ref[:, 0:memory, :].reshape(count, HEAD)
    values = got_ref[:, memory : 2 * memory, :].reshape(count, HEAD)
    for at, column in enumerate((x, (x + NX - 1) % NX)):
        first = 2 * memory + at * beams
        rows = got_ref[:, first : first + beams, :].reshape(NZ * beams, HEAD)
        scores = lax.dot_general(
            rows, keys, (((1,), (1,)), ((), ())), preferred_element_type=F32
        )
        masked = []
        for src in range(NZ):
            mine = user == owner_ref[src * NX + column]
            bias = jnp.where(mine & valid, 0.0, -1e30)
            masked.append(scores[src * beams : (src + 1) * beams] * HEAD ** (-0.5) + bias)
        scores = jnp.concatenate(masked, axis=0)
        top = jnp.max(scores, axis=-1, keepdims=True)
        expo = jnp.exp(scores - top)
        total = jnp.sum(expo, axis=-1, keepdims=True)
        weights = (expo * (1.0 / total)).astype(BF)
        mixed = jnp.dot(weights, values, preferred_element_type=F32).astype(BF)
        out_ref[:, at * beams : (at + 1) * beams, :] = mixed.reshape(NZ, beams, HEAD)


def attend(got, counts, owner, beams):
    return pl.pallas_call(
        attend_kernel,
        in_specs=[
            pl.BlockSpec(memory_space=pltpu.SMEM),
            pl.BlockSpec(memory_space=pltpu.VMEM),
            pl.BlockSpec(memory_space=pltpu.VMEM),
        ],
        out_shape=jax.ShapeDtypeStruct((NZ, 2 * beams, HEAD), BF),
        cost_estimate=pl.CostEstimate(
            flops=300_000_000, bytes_accessed=1_000_000, transcendentals=600_000
        ),
        compiler_params=pltpu.CompilerParams(vmem_limit_bytes=12 * 2**20),
        name="attend",
    )(owner, got, *in_hbm(counts))


def preload_kernel(source_ref, target_ref, sem):
    copy = pltpu.make_async_copy(source_ref, target_ref, sem)
    copy.start()
    copy.wait()


def preload(weight):
    return pl.pallas_call(
        preload_kernel,
        in_specs=[pl.BlockSpec(memory_space=pl.ANY)],
        out_specs=pl.BlockSpec(memory_space=pltpu.VMEM),
        out_shape=jax.ShapeDtypeStruct(weight.shape, weight.dtype),
        scratch_shapes=[pltpu.SemaphoreType.DMA],
        cost_estimate=pl.CostEstimate(flops=0, bytes_accessed=4 * 2**20, transcendentals=0),
        compiler_params=pltpu.CompilerParams(vmem_limit_bytes=4 * 2**20),
        name="preload",
    )(*in_hbm(weight))


def experts_kernel(*refs):
    *ins, up_ref, down_ref = refs[: len(refs) // 2 + 1]
    outs = refs[len(refs) // 2 + 1 :]
    rows = jnp.concatenate([ref[...] for ref in ins], axis=0)
    hidden = jnp.dot(rows, up_ref[...], preferred_element_type=F32)
    hidden = (hidden / (1.0 + jnp.exp(-hidden))).astype(BF)
    total = jnp.dot(hidden, down_ref[...], preferred_element_type=F32).astype(BF)
    size = ins[0].shape[0]
    for index, out_ref in enumerate(outs):
        out_ref[...] = total[index * size : (index + 1) * size]


def experts(blocks, up, down):
    count = len(blocks)
    size = count * blocks[0].shape[0]
    width, hidden = up.shape
    return pl.pallas_call(
        experts_kernel,
        in_specs=[pl.BlockSpec(memory_space=pltpu.VMEM)] * (count + 2),
        out_shape=[jax.ShapeDtypeStruct(block.shape, BF) for block in blocks],
        cost_estimate=pl.CostEstimate(
            flops=400 * size * width * hidden,
            bytes_accessed=4 * width * hidden + 4 * size * width,
            transcendentals=size * hidden,
        ),
        compiler_params=pltpu.CompilerParams(vmem_limit_bytes=10 * 2**20),
        name="experts",
    )(*blocks, up, down)


def on_device(
    queries, keys, values, kv_count, beam_user, routes, route_gate, norm_gain, w_up, w_down
):
    beams, width = queries.shape
    users, shard_len, _ = keys.shape
    shard = users * shard_len

    routes, route_gate = routes.T, route_gate.T

    size = NZ * CAP
    packed = pack_rows(queries, routes, norm_gain)
    for_right, for_left, for_far, mine = split_heads(
        queries, keys.reshape(shard, width), values.reshape(shard, width)
    )
    left, right, far = to_right(for_right), to_left(for_left), to_far(for_far)
    block = along_z(packed, FIRST).reshape(size, width)
    w_up, _ = lax.optimization_barrier((w_up, for_far))
    w_up = preload(w_up)
    block, far, w_up = lax.optimization_barrier((block, far, w_up))
    block_f, block_l, block_r = to_far(block), to_right(block), to_left(block)
    w_down, _ = lax.optimization_barrier((w_down, block))
    w_down = preload(w_down)
    (part,) = experts([block], w_up, w_down)

    got = along_z(pack_heads(mine, left, right, far))
    mixed = along_z(attend(got, kv_count, beam_user, beams))
    other = to_left(mixed)

    (part_f,) = experts([block_f], w_up, w_down)
    from_f = to_far(part_f)
    block_l, block_r, part, _ = lax.optimization_barrier((block_l, block_r, part, part_f))
    part_l, part_r = experts([block_l, block_r], w_up, w_down)
    from_r, from_l = to_left(part_l), to_right(part_r)
    ret = along_z(finish(own_and_far(part, from_f), from_l, from_r), LAST)
    context, routed = combine(ret, mixed, other, routes, route_gate, beams, width)
    return (context, routed)


def solution(mesh):
    return jax.shard_map(
        on_device,
        mesh=mesh,
        in_specs=(
            P(("user", "dev"), None),
            P("user", "dev", None),
            P("user", "dev", None),
            P("user", None),
            P("user"),
            P(("user", "dev"), None),
            P(("user", "dev"), None),
            P(),
            P(None, "dev"),
            P("dev", None),
        ),
        out_specs=(P(("user", "dev"), None), P(("user", "dev"), None)),
        check_vma=False,
    )
```
